256 devices in a mesh: grp: 4 (over x_lo, core), blk: 4 (over y), head: 16 (over z, x_hi).
Axes of the slice: x: 4 (x_hi: 2, x_lo: 2; x = x_hi * 2 + x_lo), y: 4, z: 8, core: 2. Of those that a mesh axis runs over, the one named last changes fastest.
Arguments:
- enc_states: bfloat16 [512, 4096], P(('grp', 'blk', 'head')), may hold values from -6 to 6
- image_count: int32 [4], P('grp'), may hold values from 1 to 64
- prompt_count: int32 [4], P('grp'), may hold values from 1 to 64
- enc_gain: float32 [4096], replicated, may hold values from 0.5 to 2
- enc_gate: bfloat16 [4096, 14336], P(None, ('blk', 'head')), may hold values from -0.09375 to 0.09375
- enc_up: bfloat16 [4096, 14336], P(None, ('blk', 'head')), may hold values from -0.09375 to 0.09375
- enc_down: bfloat16 [14336, 4096], P(('blk', 'head')), may hold values from -0.046875 to 0.046875
- final_gain: float32 [4096], P(('blk', 'head')), may hold values from 0.5 to 2
- w_in: bfloat16 [4096, 3072], P(('blk', 'head')), may hold values from -0.09375 to 0.09375
- mod_text: float32 [4, 2, 3072], P('grp'), may hold values from -2.5 to 2.5
- mod_video: float32 [4, 2, 3072], P('grp'), may hold values from -2.5 to 2.5
- w_kv_text: bfloat16 [3072, 16, 256], P(None, 'head'), may hold values from -0.109375 to 0.109375
- w_qkv: bfloat16 [3072, 16, 384], P(None, 'head'), may hold values from -0.07252963 to 0.07252963
- query_gain: float32 [128], replicated, may hold values from 0.5 to 6
- key_gain: float32 [128], replicated, may hold values from 0.5 to 6
- text_key_gain: float32 [128], replicated, may hold values from 0.5 to 3
- video_states: bfloat16 [32768, 3072], P(('grp', 'blk', 'head')), may hold values from -6 to 6
Outputs:
- attended: bfloat16 [32768, 2048], P(('grp', 'blk', 'head'))
The draws below stay inside these ranges and needn't reach their ends.
All inputs are finite; a program needn't handle non-finite values.
Results may differ from the reference program's by a relative error of at most 0.005.
The reference program's roundings to bfloat16 on the way count: a program that leaves them out, or rounds other values in their place, can miss the bound.
Values may be sent and summed in bfloat16 or wider, within the bound.
A program may use at most 192 MiB of HBM per device.

```python
import math
import jax
import jax.numpy as jnp
from jax import lax

D = 3072
HD = 128
ED = 4096
EFF = 14336
IMG_ROWS = 64
TXT_ROWS = 64
HEADS = 16
REQ = 4
LC = 128
VID = 8192


def draw_w_qkv(key, part):
    key = jax.random.fold_in(key, 7)
    base_key = jax.random.fold_in(key, 0)
    weights = jnp.clip(jax.random.normal(base_key, (D, HEADS, 3 * HD), jnp.float32), -4.0, 4.0)
    return (weights * D ** (-0.5)).astype(jnp.bfloat16)


def draw_query_gain(key, part):
    key = jax.random.fold_in(key, 11)
    gains = jnp.exp(jax.random.uniform(key, (HD,), jnp.float32, math.log(0.5), math.log(3.0)))
    return gains


def draw_key_gain(key, part):
    key = jax.random.fold_in(key, 12)
    gains = jnp.exp(jax.random.uniform(key, (HD,), jnp.float32, math.log(0.5), math.log(3.0)))
    return gains


def draw_video_states(key, part):
    key = jax.random.fold_in(key, 5)
    base_key = jax.random.fold_in(key, 0)
    states = jax.random.normal(base_key, (REQ, VID, D), jnp.float32)
    return jnp.clip(states, -6.0, 6.0).reshape(REQ * VID, D).astype(jnp.bfloat16)


def place_ends(result, rng, least, largest):
    spot = [jax.random.randint(jax.random.fold_in(rng, axis), (), 0, length) for axis, length in enumerate(result.shape)]
    main_axis = result.shape.index(max(result.shape))
    next_to = spot[:main_axis] + [(spot[main_axis] + 1) % result.shape[main_axis]] + spot[main_axis + 1:]
    return result.at[tuple(spot)].set(least).at[tuple(next_to)].set(largest)


def steps_of(key, shape, pieces, least, high):
    factor_of = 1.0
    for axis_at, shards_of in pieces:
        steps = jax.random.uniform(jax.random.fold_in(jax.random.fold_in(key, 6), axis_at), (shards_of,), jnp.float32, least / len(pieces), high / len(pieces))
        factor_of = factor_of * jnp.repeat(jnp.exp(steps), shape[axis_at] // shards_of).reshape((-1,) + (1,) * (len(shape) - 1 - axis_at))
    return factor_of


def noise(stream_key, dims, scale, most, shards=(), kind=jnp.bfloat16):
    values = scale * jax.random.normal(stream_key, dims, jnp.float32)
    if shards:
        values = values * steps_of(stream_key, dims, shards, -0.22, 0.18)
    return jnp.clip(values, -most, most).astype(kind)


def setup_inputs(seed: int = 0) -> dict:
    streams_of = jax.random.split(jax.random.key(seed), 18)
    enc_states = noise(streams_of[0], (REQ * LC, ED), 1.0, 6.0, ((0, 256),))
    image_count = place_ends(jax.random.randint(streams_of[1], (REQ,), 1, IMG_ROWS + 1), jax.random.fold_in(streams_of[1], 1), 1, IMG_ROWS).astype(jnp.int32)
    prompt_count = place_ends(jax.random.randint(streams_of[2], (REQ,), 1, TXT_ROWS + 1), jax.random.fold_in(streams_of[2], 1), 1, TXT_ROWS).astype(jnp.int32)
    enc_gain = jnp.clip(jnp.exp(jax.random.uniform(streams_of[3], (ED,), jnp.float32, math.log(0.5), math.log(2.0))), 0.5, 2.0)
    enc_gate = noise(streams_of[4], (ED, EFF), ED ** -0.5, 0.09375, ((1, 64),))
    enc_up = noise(streams_of[5], (ED, EFF), ED ** -0.5, 0.09375, ((1, 64),))
    enc_down = noise(streams_of[6], (EFF, ED), EFF ** -0.5, 0.046875, ((0, 64),))
    final_gain = jnp.clip(jnp.exp(math.log(2.0) - 1.3862944 * jax.random.uniform(streams_of[7], (ED,), jnp.float32) ** steps_of(streams_of[7], (ED,), ((0, 64),), -0.2, 0.2)), 0.5, 2.0)
    w_in = noise(streams_of[8], (ED, D), ED ** -0.5, 0.09375, ((0, 64),))
    mod_text = noise(streams_of[9], (REQ, 2, D), 0.5, 2.5, ((0, 4),), jnp.float32)
    mod_video = noise(streams_of[10], (REQ, 2, D), 0.5, 2.5, ((0, 4),), jnp.float32)
    w_kv_text = noise(streams_of[11], (D, HEADS, 2 * HD), D ** -0.5, 0.109375, ((1, 16),))
    w_qkv = draw_w_qkv(jax.random.fold_in(streams_of[17], 71), 0)
    query_gain = draw_query_gain(jax.random.fold_in(streams_of[17], 71), 0)
    key_gain = draw_key_gain(jax.random.fold_in(streams_of[17], 71), 0)
    text_key_gain = jnp.clip(jnp.exp(jax.random.uniform(streams_of[15], (HD,), jnp.float32, math.log(0.5), math.log(3.0))), 0.5, 3.0)
    video_states = draw_video_states(jax.random.fold_in(streams_of[17], 71), 0)
    return {"enc_states": enc_states, "image_count": image_count, "prompt_count": prompt_count, "enc_gain": enc_gain, "enc_gate": enc_gate, "enc_up": enc_up, "enc_down": enc_down, "final_gain": final_gain, "w_in": w_in, "mod_text": mod_text, "mod_video": mod_video, "w_kv_text": w_kv_text, "w_qkv": w_qkv, "query_gain": query_gain, "key_gain": key_gain, "text_key_gain": text_key_gain, "video_states": video_states}


epsilon = 1e-06
negative = -1e+30

def rms_norm(values, scale):
    return values * lax.rsqrt(lax.optimization_barrier(jnp.mean(values * values, axis=-1, keepdims=True)) + epsilon) * scale

def layer_norm(values):
    center = values - lax.optimization_barrier(jnp.mean(values, axis=-1, keepdims=True))
    return center * lax.rsqrt(lax.optimization_barrier(jnp.mean(center * center, axis=-1, keepdims=True)) + epsilon)

def reference(enc_states, image_count, prompt_count, enc_gain, enc_gate, enc_up, enc_down, final_gain, w_in, mod_text, mod_video, w_kv_text, w_qkv, query_gain, key_gain, text_key_gain, video_states):
    enc_float = enc_states.astype(jnp.float32)
    normed = rms_norm(enc_float, enc_gain).astype(jnp.bfloat16)
    gate = jnp.dot(normed, enc_gate, preferred_element_type=jnp.float32)
    upward = jnp.dot(normed, enc_up, preferred_element_type=jnp.float32)
    hidden = (jax.nn.silu(gate) * upward).astype(jnp.bfloat16)
    enc_out = enc_float + jnp.dot(hidden, enc_down, preferred_element_type=jnp.float32)
    mean_square = lax.optimization_barrier(jnp.mean(enc_out * enc_out, axis=-1))
    scaled = (enc_out * final_gain).astype(jnp.bfloat16)
    condition = jnp.dot(scaled, w_in, preferred_element_type=jnp.float32) * lax.rsqrt(mean_square + epsilon)[:, None]
    video_weights = jnp.transpose(w_qkv, (1, 0, 2))
    text_weights = jnp.transpose(w_kv_text, (1, 0, 2))
    results = []
    for request in range(REQ):
        cond_rows = condition[request * LC:(request + 1) * LC]
        cond_mod = (layer_norm(cond_rows) * (1.0 + mod_text[request, 1]) + mod_text[request, 0]).astype(jnp.bfloat16)
        video_rows = video_states[request * VID:(request + 1) * VID].astype(jnp.float32)
        video_mod = (layer_norm(video_rows) * (1.0 + mod_video[request, 1]) + mod_video[request, 0]).astype(jnp.bfloat16)
        rows = jnp.arange(LC, dtype=jnp.int32)
        live = jnp.where(rows < IMG_ROWS, rows < image_count[request], rows - IMG_ROWS < prompt_count[request])
        allowed = jnp.concatenate([jnp.ones((VID,), dtype=bool), live])

        def one_head(weights_pair):
            video_weight, text_weight = weights_pair
            mixed = jnp.dot(video_mod, video_weight, preferred_element_type=jnp.float32)
            queries = rms_norm(mixed[:, :HD], query_gain).astype(jnp.bfloat16)
            keys = rms_norm(mixed[:, HD:2 * HD], key_gain).astype(jnp.bfloat16)
            values = mixed[:, 2 * HD:].astype(jnp.bfloat16)
            text_kv = jnp.dot(cond_mod, text_weight, preferred_element_type=jnp.float32)
            text_keys = rms_norm(text_kv[:, :HD], text_key_gain).astype(jnp.bfloat16)
            text_values = text_kv[:, HD:].astype(jnp.bfloat16)
            all_keys = jnp.concatenate([keys, text_keys], axis=0)
            all_values = jnp.concatenate([values, text_values], axis=0)
            scores = jnp.dot(queries, all_keys.T, preferred_element_type=jnp.float32) * HD ** (-0.5)
            scores = jnp.where(allowed[None, :], scores, negative)
            highest = lax.optimization_barrier(jnp.max(scores, axis=-1, keepdims=True))
            weights = jnp.exp(scores - highest)
            total = lax.optimization_barrier(jnp.sum(weights, axis=-1, keepdims=True))
            output = jnp.dot(weights.astype(jnp.bfloat16), all_values, preferred_element_type=jnp.float32) / total
            return output.astype(jnp.bfloat16)
        per_head = lax.map(one_head, (video_weights, text_weights))
        results.append(jnp.transpose(per_head, (1, 0, 2)).reshape(VID, HEADS * HD))
    return jnp.concatenate(results, axis=0)
```

```python
import functools

import jax
import jax.numpy as jnp
from jax import lax
from jax.experimental import pallas as pl
from jax.experimental.pallas import tpu as pltpu
from jax.sharding import PartitionSpec as P

MESH = pl.DeviceIdType.MESH
EPS = 1e-06
NEG = -1e30
IMG_ROWS = 64
F32 = jnp.float32
BF16 = jnp.bfloat16
HD = 128
D = 3072
ED = 4096
STEP_CHUNKS = ((0, 1), (1, 2), (3, 2), (5, 2), (7, 1))
N_COPIES = 96


def dot(a, b):
    return jnp.dot(a, b, preferred_element_type=F32)


def dot_t(a, b):
    return lax.dot_general(a, b, (((1,), (1,)), ((), ())), preferred_element_type=F32)


def rms(values, gain):
    return values * lax.rsqrt(jnp.mean(values * values, axis=-1, keepdims=True) + EPS) * gain


class Links:
    def __init__(self, send, recv):
        self.send, self.recv, self.count, self.started = send, recv, 0, []

    def start(self, src, dst, device):
        copy = pltpu.make_async_remote_copy(
            src_ref=src,
            dst_ref=dst,
            send_sem=self.send.at[self.count],
            recv_sem=self.recv.at[self.count],
            device_id=device,
            device_id_type=MESH,
        )
        copy.start()
        self.count += 1
        self.started.append(copy)
        return copy

    def drain(self):
        for copy in self.started:
            copy.wait_send()


def front_kernel(
    enc_own, video, mod_video, mod_text, enc_gain, final_gain, query_gain, key_gain, text_gain,
    w_qkv, gate_t, up_t, down, w_in, w_kv,
    q_out, kv_out, text_out,
    tok0, tok1, tok2, tok3, tok4, w_two, g_v, u_v, d_v, wi_v, wk_v,
    xq, xkv, granules, rows_v, normed_v, term, r_term, part, r_part, part_x, r_x,
    proj, r_proj, proj_z, r_projz, proj_x, r_projx, cond,
    send, recv, local_sem,
):
    g, y, h = lax.axis_index("grp"), lax.axis_index("blk"), lax.axis_index("head")
    z, X = h // 2, h % 2
    core = g % 2
    z_at = lambda dz: (g, y, ((z + dz) % 8) * 2 + X)
    y_at = lambda dy: (g, (y + dy) % 4, h)
    x_at = (g, y, z * 2 + (1 - X))
    w_at = ((g + 2) % 4, y, z * 2 + (1 - X))
    core_at = (g + 1 - 2 * core, y, h)
    peers = [z_at(i) for i in range(1, 8)] + [y_at(i) for i in range(1, 4)] + [x_at, w_at, core_at]

    loads = [
        pltpu.make_async_copy(src, dst, local_sem.at[i])
        for i, (src, dst) in enumerate(
            [(w_qkv, w_two.at[0]), (gate_t, g_v), (up_t, u_v), (down, d_v), (w_in, wi_v), (w_kv, wk_v)]
        )
    ]
    for load in loads:
        load.start()

    barrier = pltpu.get_barrier_semaphore()
    for peer in peers:
        pl.semaphore_signal(barrier, inc=1, device_id=peer, device_id_type=MESH)
    pl.semaphore_wait(barrier, len(peers))

    links = Links(send, recv)

    granules[y, X, z] = enc_own[...]
    enc_z = [
        links.start(granules.at[y, X, z], granules.at[y, X, z], z_at(i)) for i in range(1, 8)
    ]

    scale, shift = 1.0 + mod_video[1:2, :], mod_video[0:1, :]

    def modulate(i, _):
        at = pl.ds(pl.multiple_of(i * 16, 16), 16)
        v = video[at, :].astype(F32)
        c = v - jnp.mean(v, axis=-1, keepdims=True)
        n = c * lax.rsqrt(jnp.mean(c * c, axis=-1, keepdims=True) + EPS)
        tok0[at, :] = (n * scale + shift).astype(BF16)
        return 0

    lax.fori_loop(0, 8, modulate, 0)
    toks = [tok0, tok1, tok2, tok3, tok4]

    def ring(step):
        if step == 1:
            up, down_ = tok0, tok0
        else:
            up, down_ = toks[step - 1].at[0:128], toks[step - 1].at[128:256]
        if step < 4:
            return [
                links.start(up, toks[step].at[0:128], z_at(1)),
                links.start(down_, toks[step].at[128:256], z_at(7)),
            ]
        return [
            links.start(toks[3].at[0:64], tok4.at[0:64], z_at(1)),
            links.start(toks[3].at[192:256], tok4.at[64:128], z_at(7)),
        ]

    arrivals = [None, ring(1)]
    half = pl.ds(pl.multiple_of(core * (D // 2), D // 2), D // 2)
    w_half = links.start(w_qkv.at[half], w_two.at[1, half], w_at)

    q_gain, k_gain = query_gain[...], key_gain[...]

    def project(step, which):
        first, count = STEP_CHUNKS[step]
        mixed = dot(toks[step][...], w_two[which])
        q = rms(mixed[:, :HD], q_gain).astype(BF16)
        k = rms(mixed[:, HD : 2 * HD], k_gain).astype(BF16)
        v = mixed[:, 2 * HD :].astype(BF16)
        for i in range(count):
            at = slice(i * 128, (i + 1) * 128)
            if which == 0:
                q_out[0, first + i] = q[at]
                kv_out[0, 0, first + i, 0] = k[at]
                kv_out[0, 0, first + i, 1] = v[at]
            else:
                xq[first + i] = q[at]
                xkv[first + i, 0] = k[at]
                xkv[first + i, 1] = v[at]

    y_copies, x_copies = [], {}

    def spread(step, x_rel):
        first, count = STEP_CHUNKS[step]
        for dy in (1, 3, 2):
            y_copies.append(
                links.start(
                    kv_out.at[0, x_rel, pl.ds(first, count)],
                    kv_out.at[4 - dy, x_rel, pl.ds(first, count)],
                    y_at(dy),
                )
            )

    def own_head(step):
        project(step, 0)
        spread(step, 0)

    def other_head(step):
        first, count = STEP_CHUNKS[step]
        project(step, 1)
        x_copies[step] = [
            links.start(xq.at[pl.ds(first, count)], q_out.at[1, pl.ds(first, count)], x_at),
            links.start(
                xkv.at[pl.ds(first, count)], kv_out.at[0, 1, pl.ds(first, count)], x_at
            ),
        ]

    def pass_on(step):
        for copy in x_copies[step]:
            copy.wait_recv()
        spread(step, 1)

    def arrive(step):
        for copy in arrivals[step]:
            copy.wait_recv()
        if step < 4:
            arrivals.append(ring(step + 1))

    for copy in enc_z:
        copy.wait_recv()
    enc_x = links.start(granules.at[y, X], granules.at[y, X], x_at)
    loads[0].wait()
    own_head(0)
    enc_x.wait_recv()
    enc_y = [links.start(granules.at[y], granules.at[y], y_at(i)) for i in (1, 3, 2)]

    for copy in enc_y:
        copy.wait_recv()
    out_at = lax.broadcasted_iota(jnp.int32, (256, 256), 0)
    in_at = lax.broadcasted_iota(jnp.int32, (256, 256), 1)
    order = (in_at == (out_at % 32) * 8 + out_at // 32).astype(F32).astype(BF16)
    for b in range(4):
        sorted_rows = dot(order, granules[b].reshape(256, 512)).astype(BF16)
        for j in range(8):
            rows_v[32 * b : 32 * b + 32, 512 * j : 512 * j + 512] = sorted_rows[32 * j : 32 * j + 32]

    def normalize(i, _):
        at = pl.ds(pl.multiple_of(i * 16, 16), 16)
        v = rows_v[at, :].astype(F32)
        normed_v[at, :] = rms(v, enc_gain[...]).astype(BF16)
        return 0

    lax.fori_loop(0, 8, normalize, 0)
    loads[1].wait()
    loads[2].wait()
    gate = dot_t(normed_v[...], g_v[...])
    upward = dot_t(normed_v[...], u_v[...])
    hidden = (gate / (1.0 + jnp.exp(-gate)) * upward).astype(BF16)
    loads[3].wait()
    for b in range(4):
        term[b] = dot(hidden, d_v[:, 1024 * b : 1024 * b + 1024]).astype(BF16)
    enc_ry = [links.start(term.at[(y + i) % 4], r_term.at[i - 1], y_at(i)) for i in (1, 3, 2)]

    arrive(1)
    own_head(1)

    for copy in enc_ry:
        copy.wait_recv()
    total = term[y].astype(F32)
    for i in range(3):
        total = total + r_term[i].astype(F32)
    for i in range(8):
        part[i] = total[:, 128 * i : 128 * i + 128].astype(BF16)
    enc_rz = [links.start(part.at[(z + i) % 8], r_part.at[i - 1], z_at(i)) for i in range(1, 8)]

    w_half.wait_recv()
    w_core = links.start(w_two.at[1, half], w_two.at[1, half], core_at)

    for copy in enc_rz:
        copy.wait_recv()
    total = part[z].astype(F32)
    for i in range(7):
        total = total + r_part[i].astype(F32)
    part_x[...] = total
    enc_rx = links.start(part_x, r_x, x_at)

    w_core.wait_recv()
    other_head(0)
    other_head(1)

    enc_rx.wait_recv()
    column = pl.multiple_of(y * 1024 + z * 128, 128)
    enc_out = total + r_x[...] + rows_v[:, pl.ds(column, 128)].astype(F32)
    own = jnp.where(X == 0, enc_out[:, :64], enc_out[:, 64:])
    squares = jnp.sum(own * own, axis=-1, keepdims=True)
    scaled = (own * final_gain[...]).astype(BF16)
    loads[4].wait()
    wide = jnp.broadcast_to(squares, (128, 128)).astype(BF16)
    for b in range(4):
        proj[b, :, D:] = wide[32 * b : 32 * b + 32]
    for i in range(6):
        product = dot(scaled, wi_v[:, 512 * i : 512 * i + 512]).astype(BF16)
        for b in range(4):
            proj[b, :, 512 * i : 512 * i + 512] = product[32 * b : 32 * b + 32]
    ref_y = [links.start(proj.at[(y + i) % 4], r_proj.at[i - 1], y_at(i)) for i in (1, 3, 2)]

    arrive(2)
    own_head(2)
    pass_on(0)
    pass_on(1)

    for copy in ref_y:
        copy.wait_recv()
    total = proj[y].astype(F32)
    for i in range(3):
        total = total + r_proj[i].astype(F32)
    for i in range(8):
        proj_z[i, :, :384] = total[:, 384 * i : 384 * i + 384].astype(BF16)
        proj_z[i, :, 384:] = total[:, D:].astype(BF16)
    ref_z = [links.start(proj_z.at[(z + i) % 8], r_projz.at[i - 1], z_at(i)) for i in range(1, 8)]

    other_head(2)

    for copy in ref_z:
        copy.wait_recv()
    total = proj_z[z].astype(F32)
    for i in range(7):
        total = total + r_projz[i].astype(F32)
    proj_x[...] = total
    ref_x = links.start(proj_x, r_projx, x_at)

    arrive(3)
    own_head(3)
    pass_on(2)

    ref_x.wait_recv()
    total = total + r_projx[...]
    cond[z] = (total[:, :384] * lax.rsqrt(total[:, 384:385] / ED + EPS)).astype(BF16)
    ref_all = [links.start(cond.at[z], cond.at[z], z_at(i)) for i in range(1, 8)]

    other_head(3)

    for copy in ref_all:
        copy.wait_recv()
    total = jnp.zeros((32, 1), F32)
    for i in range(8):
        total = total + jnp.sum(cond[i].astype(F32), axis=-1, keepdims=True)
    mean = total / D
    total = jnp.zeros((32, 1), F32)
    for i in range(8):
        c = cond[i].astype(F32) - mean
        total = total + jnp.sum(c * c, axis=-1, keepdims=True)
    inverse = lax.rsqrt(total / D + EPS)
    loads[5].wait()
    text = jnp.zeros((32, 256), F32)
    for i in range(8):
        at = slice(384 * i, 384 * i + 384)
        c = (cond[i].astype(F32) - mean) * inverse
        c = (c * (1.0 + mod_text[1:2, at]) + mod_text[0:1, at]).astype(BF16)
        text = text + dot(c, wk_v[at, :])
    text_out[y, 0] = rms(text[:, :HD], text_gain[...]).astype(BF16)
    text_out[y, 1] = text[:, HD:].astype(BF16)
    text_y = [links.start(text_out.at[y], text_out.at[y], y_at(i)) for i in (1, 3, 2)]

    arrive(4)
    other_head(4)
    own_head(4)
    pass_on(3)
    pass_on(4)

    for copy in text_y + y_copies:
        copy.wait_recv()
    links.drain()


def attend_kernel(q_ref, kv_ref, text_ref, bias_ref, out_ref, staged, send, recv, local_sem):
    g, y, h = lax.axis_index("grp"), lax.axis_index("blk"), lax.axis_index("head")
    z, X = h // 2, h % 2

    def peer(k):
        c, x_rel = k % 8, k // 8
        offset = (c % 2) * (8 - (c + 1) // 2) + (1 - c % 2) * (c // 2)
        return (g, y, ((z + offset) % 8) * 2 + (X + x_rel) % 2)

    barrier = pltpu.get_barrier_semaphore()
    for k in range(1, 16):
        pl.semaphore_signal(barrier, inc=1, device_id=peer(k), device_id_type=MESH)
    pl.semaphore_wait(barrier, 15)

    columns = pl.ds(pl.multiple_of(h * 128, 128), 128)

    def deliver(k):
        return pltpu.make_async_remote_copy(
            src_ref=staged.at[k],
            dst_ref=out_ref.at[:, columns],
            send_sem=send.at[k],
            recv_sem=recv.at[k],
            device_id=peer(k),
            device_id_type=MESH,
        )

    factor = HD ** (-0.5) * 1.4426950408889634
    ones = jnp.ones((1024, 128), BF16)

    def tile(i, _):
        t = 7 - i
        x_rel, c = t // 4, (t % 4) * 2
        q = q_ref[x_rel, pl.ds(c, 2)].reshape(256, 128)

        def scores_of(n):
            if n == 8:
                keys = text_ref[:, 0].reshape(128, 128)
                return dot_t(q, keys) * factor + bias_ref[...]
            keys = kv_ref[n // 2, n % 2, :, 0].reshape(1024, 128)
            return dot_t(q, keys) * factor

        highest = acc = None
        s = scores_of(0)
        for n in range(9):
            following = scores_of(n + 1) if n < 8 else None
            top = jnp.max(s, axis=-1, keepdims=True)
            if n > 0:
                top = jnp.maximum(highest, top)
            weights = jnp.exp2(s - top).astype(BF16)
            if n == 8:
                values = jnp.concatenate([text_ref[:, 1].reshape(128, 128), ones[:128]], axis=1)
            else:
                values = jnp.concatenate(
                    [kv_ref[n // 2, n % 2, :, 1].reshape(1024, 128), ones], axis=1
                )
            product = dot(weights, values)
            acc = product if n == 0 else acc * jnp.exp2(highest - top) + product
            highest = top
            s = following
        out = (acc[:, :HD] / acc[:, HD:]).astype(BF16)
        k = t * 2
        staged[k] = out[:128]
        staged[k + 1] = out[128:]
        deliver(k + 1).start()

        @pl.when(t > 0)
        def _():
            deliver(k).start()

        return 0

    lax.fori_loop(0, 8, tile, 0)
    own = pltpu.make_async_copy(staged.at[0], out_ref.at[:, columns], local_sem)
    own.start()
    own.wait()
    for k in range(1, 16):
        deliver(k).wait()


def local(
    enc_states, image_count, prompt_count, enc_gain, enc_gate, enc_up, enc_down, final_gain, w_in,
    mod_text, mod_video, w_kv_text, w_qkv, query_gain, key_gain, text_key_gain, video_states,
):
    vmem, hbm = pl.BlockSpec(memory_space=pltpu.VMEM), pl.BlockSpec(memory_space=pl.ANY)
    row = lambda v: v.reshape(1, -1)
    q, kv, text = pl.pallas_call(
        front_kernel,
        out_shape=[
            jax.ShapeDtypeStruct((2, 8, 128, 128), BF16),
            jax.ShapeDtypeStruct((4, 2, 8, 2, 128, 128), BF16),
            jax.ShapeDtypeStruct((4, 2, 32, 128), BF16),
        ],
        in_specs=[vmem] * 9 + [hbm] * 6,
        out_specs=[vmem] * 3,
        scratch_shapes=[
            pltpu.VMEM((128, D), BF16),
            pltpu.VMEM((256, D), BF16),
            pltpu.VMEM((256, D), BF16),
            pltpu.VMEM((256, D), BF16),
            pltpu.VMEM((128, D), BF16),
            pltpu.VMEM((2, D, 3 * HD), BF16),
            pltpu.VMEM((224, ED), BF16),
            pltpu.VMEM((224, ED), BF16),
            pltpu.VMEM((224, ED), BF16),
            pltpu.VMEM((64, D), BF16),
            pltpu.VMEM((D, 2 * HD), BF16),
            pltpu.VMEM((8, 128, 128), BF16),
            pltpu.VMEM((8, 2, 128, 128), BF16),
            pltpu.VMEM((4, 2, 8, 16, 512), BF16),
            pltpu.VMEM((128, ED), BF16),
            pltpu.VMEM((128, ED), BF16),
            pltpu.VMEM((4, 128, 1024), BF16),
            pltpu.VMEM((3, 128, 1024), BF16),
            pltpu.VMEM((8, 128, 128), BF16),
            pltpu.VMEM((7, 128, 128), BF16),
            pltpu.VMEM((128, 128), F32),
            pltpu.VMEM((128, 128), F32),
            pltpu.VMEM((4, 32, D + 128), BF16),
            pltpu.VMEM((3, 32, D + 128), BF16),
            pltpu.VMEM((8, 32, 512), BF16),
            pltpu.VMEM((7, 32, 512), BF16),
            pltpu.VMEM((32, 512), F32),
            pltpu.VMEM((32, 512), F32),
            pltpu.VMEM((8, 32, 384), BF16),
            pltpu.SemaphoreType.DMA((N_COPIES,)),
            pltpu.SemaphoreType.DMA((N_COPIES,)),
            pltpu.SemaphoreType.DMA((6,)),
        ],
        compiler_params=pltpu.CompilerParams(
            collective_id=0, has_side_effects=True, vmem_limit_bytes=56 * 2**20
        ),
        name="front",
    )(
        enc_states.reshape(16, 512), video_states, mod_video[0], mod_text[0], row(enc_gain),
        row(final_gain), row(query_gain), row(key_gain), row(text_key_gain),
        w_qkv[:, 0, :], enc_gate.T, enc_up.T, enc_down, w_in, w_kv_text[:, 0, :],
    )
    at = jnp.arange(128, dtype=jnp.int32)
    b, x, zz, r = at // 32, (at // 16) % 2, (at // 2) % 8, at % 2
    rows = 32 * b + 4 * zz + 2 * x + r
    live = jnp.where(rows < IMG_ROWS, rows < image_count[0], rows - IMG_ROWS < prompt_count[0])
    bias = jnp.where(live, 0.0, NEG).astype(F32).reshape(1, 128)
    return pl.pallas_call(
        attend_kernel,
        out_shape=jax.ShapeDtypeStruct((128, 2048), BF16),
        in_specs=[vmem] * 4,
        out_specs=vmem,
        scratch_shapes=[
            pltpu.VMEM((16, 128, 128), BF16),
            pltpu.SemaphoreType.DMA((16,)),
            pltpu.SemaphoreType.DMA((16,)),
            pltpu.SemaphoreType.DMA,
        ],
        compiler_params=pltpu.CompilerParams(
            collective_id=1, has_side_effects=True, vmem_limit_bytes=56 * 2**20
        ),
        name="attend",
    )(q, kv, text, bias)


def solution(mesh):
    placed = (
        P(("grp", "blk", "head"), None),
        P("grp"),
        P("grp"),
        P(),
        P(None, ("blk", "head")),
        P(None, ("blk", "head")),
        P(("blk", "head"), None),
        P(("blk", "head")),
        P(("blk", "head"), None),
        P("grp", None, None),
        P("grp", None, None),
        P(None, "head", None),
        P(None, "head", None),
        P(),
        P(),
        P(),
        P(("grp", "blk", "head"), None),
    )
    return jax.shard_map(
        local,
        mesh=mesh,
        in_specs=placed,
        out_specs=P(("grp", "blk", "head"), None),
        check_vma=False,
    )
```

```python
import functools

import jax
import jax.numpy as jnp
from jax import lax
from jax.experimental import pallas as pl
from jax.experimental.pallas import tpu as pltpu
from jax.sharding import PartitionSpec as P

MESH = pl.DeviceIdType.MESH
EPS = 1e-06
NEG = -1e30
IMG_ROWS = 64
F32 = jnp.float32
BF16 = jnp.bfloat16
HD = 128
D = 3072
ED = 4096
STEP_CHUNKS = ((0, 1), (1, 2), (3, 2), (5, 2), (7, 1))
N_COPIES = 120


def dot(a, b):
    return jnp.dot(a, b, preferred_element_type=F32)


def dot_t(a, b):
    return lax.dot_general(a, b, (((1,), (1,)), ((), ())), preferred_element_type=F32)


def rms(values, gain):
    return values * lax.rsqrt(jnp.mean(values * values, axis=-1, keepdims=True) + EPS) * gain


class Links:
    def __init__(self, send, recv):
        self.send, self.recv, self.count, self.started = send, recv, 0, []

    def start(self, src, dst, device):
        copy = pltpu.make_async_remote_copy(
            src_ref=src,
            dst_ref=dst,
            send_sem=self.send.at[self.count],
            recv_sem=self.recv.at[self.count],
            device_id=device,
            device_id_type=MESH,
        )
        copy.start()
        self.count += 1
        assert self.count <= N_COPIES
        self.started.append(copy)
        return copy

    def drain(self):
        for copy in self.started:
            copy.wait_send()


def block_kernel(
    image_count, prompt_count,
    enc_own, video, mod_video, mod_text, enc_gain, final_gain, query_gain, key_gain, text_gain,
    w_qkv, gate_t, up_t, down, w_in, w_kv,
    out_ref,
    q_ref, kv_ref, text_ref, acc_ref, top_ref, staged,
    tok0, tok1, tok2, tok3, tok4, w_two, g_v, u_v, d_v, wi_v, wk_v,
    xq, xkv, granules, rows_v, normed_v, term_a, r_term_a, term_b, r_term_b, half_f, half_b,
    r_half, sum_b, r_sum_b, part, r_part,
    gain_v, proj, r_proj, proj_z, r_projz, cond, cond_mod,
    send, recv, out_send, out_recv, local_sem,
):
    g, y, h = lax.axis_index("grp"), lax.axis_index("blk"), lax.axis_index("head")
    z, X = h // 2, h % 2
    core = g % 2
    z_at = lambda dz: (g, y, ((z + dz) % 8) * 2 + X)
    y_at = lambda dy: (g, (y + dy) % 4, h)
    x_at = (g, y, z * 2 + (1 - X))
    w_at = ((g + 2) % 4, y, z * 2 + (1 - X))
    core_at = (g + 1 - 2 * core, y, h)

    def owner(k):
        c, x_rel = k % 8, k // 8
        offset = (c % 2) * (8 - (c + 1) // 2) + (1 - c % 2) * (c // 2)
        return (g, y, ((z + offset) % 8) * 2 + (X + x_rel) % 2)

    peers = [owner(k) for k in range(1, 16)] + [y_at(i) for i in range(1, 4)] + [w_at, core_at]

    loads = [
        pltpu.make_async_copy(src, dst, local_sem.at[i])
        for i, (src, dst) in enumerate(
            [(w_qkv, w_two.at[0]), (gate_t, g_v), (up_t, u_v), (down, d_v), (w_in, wi_v.at[X]), (w_kv, wk_v)]
        )
    ]
    for load in loads:
        load.start()

    barrier = pltpu.get_barrier_semaphore()
    for peer in peers:
        pl.semaphore_signal(barrier, inc=1, device_id=peer, device_id_type=MESH)
    pl.semaphore_wait(barrier, len(peers))

    links = Links(send, recv)
    toks = [tok0, tok1, tok2, tok3, tok4]
    flight = {}

    def landed(name):
        for copy in flight[name]:
            copy.wait_recv()

    seen = set()

    def once(name):
        if name not in seen:
            seen.add(name)
            landed(name)

    def to_y(src, dst):
        return [links.start(src((y + i) % 4), dst(i), y_at(i)) for i in (1, 3, 2)]

    def to_z(src, dst):
        return [links.start(src((z + i) % 8), dst(i), z_at(i)) for i in (1, 7, 2, 6, 3, 5, 4)]

    def modulate_video():
        scale, shift = 1.0 + mod_video[1:2, :], mod_video[0:1, :]

        def modulate(i, _):
            at = pl.ds(pl.multiple_of(i * 16, 16), 16)
            v = video[at, :].astype(F32)
            c = v - jnp.mean(v, axis=-1, keepdims=True)
            n = c * lax.rsqrt(jnp.mean(c * c, axis=-1, keepdims=True) + EPS)
            tok0[at, :] = (n * scale + shift).astype(BF16)
            return 0

        lax.fori_loop(0, 8, modulate, 0)

    def ring(step, part):
        at, low, high = pl.ds(64 * part, 64), 64 * part, 128 + 64 * part
        back = tok0.at[at] if step == 1 else toks[step - 1].at[pl.ds(high, 64)]
        copies = []
        if step < 4 or part == 0:
            copies.append(links.start(toks[step - 1].at[at], toks[step].at[at], z_at(1)))
        if step < 4:
            copies.append(links.start(back, toks[step].at[pl.ds(high, 64)], z_at(7)))
        elif part == 1:
            copies.append(links.start(back, tok4.at[at], z_at(7)))
        flight["tok", step, part] = copies

    def arrive(step, part):
        landed(("tok", step, part))
        if step < 4:
            ring(step + 1, part)

    half = pl.ds(pl.multiple_of(core * (D // 2), D // 2), D // 2)

    def weights_x():
        flight["w_half"] = [links.start(w_qkv.at[half], w_two.at[1, half], w_at)]

    def weights_core():
        landed("w_half")
        flight["w_core"] = [links.start(w_two.at[1, half], w_two.at[1, half], core_at)]

    def project(step, which):
        first, count = STEP_CHUNKS[step]
        mixed = dot(toks[step][...], w_two[which])
        q = rms(mixed[:, :HD], query_gain[...]).astype(BF16)
        k = rms(mixed[:, HD : 2 * HD], key_gain[...]).astype(BF16)
        v = mixed[:, 2 * HD :].astype(BF16)
        for i in range(count):
            at = slice(i * 128, (i + 1) * 128)
            if which == 0:
                q_ref[0, first + i] = q[at]
                kv_ref[0, 0, first + i, 0] = k[at]
                kv_ref[0, 0, first + i, 1] = v[at]
            else:
                xq[first + i] = q[at]
                xkv[first + i, 0] = k[at]
                xkv[first + i, 1] = v[at]

    def spread(step, x_rel):
        chunks = pl.ds(*STEP_CHUNKS[step])
        if x_rel:
            landed(("x", step))
        mine = kv_ref.at[0, x_rel, chunks]
        flight["kv", step, x_rel] = [
            links.start(mine, kv_ref.at[3, x_rel, chunks], y_at(1)),
            links.start(mine, kv_ref.at[1, x_rel, chunks], y_at(3)),
        ]

    def relay(step, x_rel):
        chunks = pl.ds(*STEP_CHUNKS[step])
        landed(("kv", step, x_rel))
        far = kv_ref.at[2, x_rel, chunks]
        flight["far", step, x_rel] = [
            links.start(kv_ref.at[3, x_rel, chunks, 0], far.at[:, 0], y_at(1)),
            links.start(kv_ref.at[1, x_rel, chunks, 1], far.at[:, 1], y_at(3)),
        ]

    def own_head(step):
        if step == 0:
            loads[0].wait()
        project(step, 0)

    def other_head(step):
        once("w_core")
        chunks = pl.ds(*STEP_CHUNKS[step])
        project(step, 1)
        flight["q", step] = [links.start(xq.at[chunks], q_ref.at[1, chunks], x_at)]
        flight["x", step] = [links.start(xkv.at[chunks], kv_ref.at[0, 1, chunks], x_at)]

    def enc_z():
        rows = enc_own[...].astype(F32)
        pieces = [rows[:, 512 * j : 512 * j + 512] for j in range(8)]
        granules[y, X, z] = jnp.concatenate(pieces, axis=0).astype(BF16)
        flight["enc_z"] = to_z(lambda _: granules.at[y, X, z], lambda _: granules.at[y, X, z])

    def enc_x():
        landed("enc_z")
        flight["enc_x"] = [links.start(granules.at[y, X], granules.at[y, X], x_at)]

    def enc_y():
        landed("enc_x")
        mine = granules.at[y]
        flight["enc_y"] = [links.start(mine, mine, y_at(1)), links.start(mine, mine, y_at(3))]

    def enc_far():
        landed("enc_y")
        low, high = granules.at[(y + 3) % 4, 0], granules.at[(y + 1) % 4, 1]
        flight["enc_far"] = [links.start(low, low, y_at(1)), links.start(high, high, y_at(3))]

    def gains_x():
        gain = jnp.concatenate([final_gain[...], jnp.zeros((1, 64), F32)], axis=1)
        gain_v[X] = jnp.broadcast_to(gain, (8, 128))
        flight["gains"] = [
            links.start(gain_v.at[X], gain_v.at[X], x_at),
            links.start(w_in, wi_v.at[X], x_at),
        ]

    def feed_forward():
        landed("enc_far")
        out_at = lax.broadcasted_iota(jnp.int32, (256, 256), 0)
        in_at = lax.broadcasted_iota(jnp.int32, (256, 256), 1)
        source = out_at % 32 // 2 * 16 + out_at // 32 * 2 + out_at % 2
        order = (in_at == source).astype(F32).astype(BF16)
        for b in range(4):
            ordered = dot(order, granules[b].reshape(256, 512)).astype(BF16)
            for j in range(8):
                for x in (0, 1):
                    rows_v[64 * x + 16 * b : 64 * x + 16 * b + 16, 512 * j : 512 * j + 512] = ordered[
                        32 * j + 16 * x : 32 * j + 16 * x + 16
                    ]

        def normalize(i, _):
            at = pl.ds(pl.multiple_of(i * 16, 16), 16)
            v = rows_v[at, :].astype(F32)
            normed_v[at, :] = rms(v, enc_gain[...]).astype(BF16)
            return 0

        lax.fori_loop(0, 8, normalize, 0)
        loads[1].wait()
        loads[2].wait()
        gate = dot_t(normed_v[...], g_v[...])
        upward = dot_t(normed_v[...], u_v[...])
        hidden = (gate / (1.0 + jnp.exp(-gate)) * upward).astype(BF16)
        loads[3].wait()
        for b in range(4):
            product = dot(hidden, d_v[:, 1024 * b : 1024 * b + 1024]).astype(BF16)
            term_a[b] = product[:, :512]
            term_b[0, b] = product[:64, 512:]
            term_b[1, b] = product[64:, 512:]
        flight["sum_a"] = to_y(lambda b: term_a.at[b], lambda i: r_term_a.at[i - 1])
        flight["sum_b"] = [links.start(term_b.at[1 - X], r_term_b, x_at)]

    def sum_xa():
        landed("sum_a")
        total = term_a[y].astype(F32)
        for i in range(3):
            total = total + r_term_a[i].astype(F32)
        for x in (0, 1):
            half_f[x] = total[64 * x : 64 * x + 64]
            half_b[x] = total[64 * x : 64 * x + 64].astype(BF16)
        flight["sum_xa"] = [links.start(half_b.at[1 - X], r_half, x_at)]

    def sum_yb():
        landed("sum_b")
        for b in range(4):
            sum_b[b] = (term_b[X, b].astype(F32) + r_term_b[b].astype(F32)).astype(BF16)
        flight["sum_yb"] = to_y(lambda b: sum_b.at[b], lambda i: r_sum_b.at[i - 1])

    def sum_z():
        landed("sum_xa")
        landed("sum_yb")
        total = half_f[X] + r_half[...].astype(F32)
        for i in range(4):
            part[i] = total[:, 128 * i : 128 * i + 128].astype(BF16)
        total = sum_b[y].astype(F32)
        for i in range(3):
            total = total + r_sum_b[i].astype(F32)
        for i in range(4):
            part[4 + i] = total[:, 128 * i : 128 * i + 128].astype(BF16)
        flight["sum_z"] = to_z(lambda b: part.at[b], lambda i: r_part.at[i - 1])

    def refine():
        landed("sum_z")
        total = part[z].astype(F32)
        for i in range(7):
            total = total + r_part[i].astype(F32)
        column = pl.multiple_of(y * 1024 + z * 128, 128)
        own_rows = pl.ds(pl.multiple_of(X * 64, 64), 64)
        enc_out = total + rows_v[own_rows, pl.ds(column, 128)].astype(F32)
        squares = jnp.sum(enc_out * enc_out, axis=-1, keepdims=True)
        landed("gains")
        gain = jnp.concatenate([gain_v[0][:1, :64], gain_v[1][:1, :64]], axis=1)
        scaled = (enc_out * gain).astype(BF16)
        loads[4].wait()
        wide = jnp.broadcast_to(squares, (64, 128)).astype(BF16)
        for b in range(4):
            proj[b, :, D:] = wide[16 * b : 16 * b + 16]
        for i in range(6):
            weights = wi_v[:, :, 512 * i : 512 * i + 512].reshape(128, 512)
            product = dot(scaled, weights).astype(BF16)
            for b in range(4):
                proj[b, :, 512 * i : 512 * i + 512] = product[16 * b : 16 * b + 16]
        flight["ref_y"] = to_y(lambda b: proj.at[b], lambda i: r_proj.at[i - 1])

    def refine_z():
        landed("ref_y")
        total = proj[y].astype(F32)
        for i in range(3):
            total = total + r_proj[i].astype(F32)
        for i in range(8):
            proj_z[i, :, :384] = total[:, 384 * i : 384 * i + 384].astype(BF16)
            proj_z[i, :, 384:] = total[:, D:].astype(BF16)
        flight["ref_z"] = to_z(lambda b: proj_z.at[b], lambda i: r_projz.at[i - 1])

    def refine_all():
        landed("ref_z")
        total = proj_z[z].astype(F32)
        for i in range(7):
            total = total + r_projz[i].astype(F32)
        cond[z] = (total[:, :384] * lax.rsqrt(total[:, 384:385] / ED + EPS)).astype(BF16)
        flight["cond"] = to_z(lambda _: cond.at[z], lambda _: cond.at[z])

    def modulate_x():
        landed("cond")
        total = jnp.zeros((16, 1), F32)
        for i in range(8):
            total = total + jnp.sum(cond[i].astype(F32), axis=-1, keepdims=True)
        mean = total / D
        total = jnp.zeros((16, 1), F32)
        for i in range(8):
            c = cond[i].astype(F32) - mean
            total = total + jnp.sum(c * c, axis=-1, keepdims=True)
        inverse = lax.rsqrt(total / D + EPS)
        for i in range(8):
            at = slice(384 * i, 384 * i + 384)
            c = (cond[i].astype(F32) - mean) * inverse
            cond_mod[X, :, at] = (c * (1.0 + mod_text[1:2, at]) + mod_text[0:1, at]).astype(BF16)
        flight["cond_mod"] = [links.start(cond_mod.at[X], cond_mod.at[X], x_at)]

    def text():
        landed("cond_mod")
        loads[5].wait()
        text_kv = dot(cond_mod[...].reshape(32, D), wk_v[...])
        text_ref[y, 0] = rms(text_kv[:, :HD], text_gain[...]).astype(BF16)
        text_ref[y, 1] = text_kv[:, HD:].astype(BF16)
        flight["text"] = to_y(lambda _: text_ref.at[y], lambda _: text_ref.at[y])

    factor = HD ** (-0.5) * 1.4426950408889634

    def dead_bias():
        at = lax.broadcasted_iota(jnp.int32, (1, 128), 1)
        row = at // 32 * 32 + at // 2 % 8 * 4 + at // 16 % 2 * 2 + at % 2
        end = jnp.where(row < IMG_ROWS, image_count[0], IMG_ROWS + prompt_count[0])
        return jnp.where(row < end, 0.0, NEG)

    def attend(i, tiles, fresh, last):
        q = q_ref[:, i].reshape(256, 128)
        tiles = list(tiles) + (["text"] if last else [])

        def scores_of(n):
            if n == "text":
                return dot_t(q, text_ref[:, 0].reshape(128, 128)) * factor + dead_bias()
            return dot_t(q, kv_ref[:, :, n, 0].reshape(1024, 128)) * factor

        def values_of(n):
            if n == "text":
                v = text_ref[:, 1].reshape(128, 128)
            else:
                v = kv_ref[:, :, n, 1].reshape(1024, 128)
            return jnp.concatenate([v, jnp.ones(v.shape, BF16)], axis=1)

        highest = acc = None
        if not fresh:
            highest, acc = top_ref[i][:, :1], acc_ref[i]
        s = scores_of(tiles[0])
        for at, n in enumerate(tiles):
            following = scores_of(tiles[at + 1]) if at + 1 < len(tiles) else None
            top = jnp.max(s, axis=-1, keepdims=True)
            if highest is not None:
                top = jnp.maximum(highest, top)
            product = dot(jnp.exp2(s - top).astype(BF16), values_of(n))
            acc = product if highest is None else acc * jnp.exp2(highest - top) + product
            highest, s = top, following
        if not last:
            top_ref[i] = jnp.broadcast_to(highest, (256, 128))
            acc_ref[i] = acc
            return
        out = (acc[:, :HD] / acc[:, HD:]).astype(BF16)
        staged[i] = out[:128]
        staged[8 + i] = out[128:]
        deliver(8 + i).start()

        @pl.when(i > 0)
        def _():
            deliver(i).start()

    def queries(first, end, tiles, fresh, last=False):
        def body(i, _):
            attend(end - 1 - i, tiles, fresh, last)
            return 0

        lax.fori_loop(0, end - first, body, 0)

    def attend_to(first, end, key_first, key_end, last=False):
        for step, (chunk, _) in enumerate(STEP_CHUNKS):
            if chunk < key_end:
                once(("far", step, 0))
                once(("far", step, 1))
            if chunk < end:
                once(("q", step))
        if last:
            once("text")
        queries(first, end, range(key_first, key_end), key_first == 0, last)

    columns = pl.ds(pl.multiple_of(h * 128, 128), 128)

    def deliver(k):
        return pltpu.make_async_remote_copy(
            src_ref=staged.at[k],
            dst_ref=out_ref.at[:, columns],
            send_sem=out_send.at[k],
            recv_sem=out_recv.at[k],
            device_id=owner(k),
            device_id_type=MESH,
        )

    def finish():
        own = pltpu.make_async_copy(staged.at[0], out_ref.at[:, columns], local_sem.at[6])
        own.start()
        own.wait()
        links.drain()
        for k in range(1, 16):
            deliver(k).wait()

    stages = locals()
    for name, *step in PLAN:
        stages[name](*step)


PLAN = (
    ("enc_z",), ("modulate_video",), ("ring", 1, 0), ("own_head", 0), ("spread", 0, 0),
    ("ring", 1, 1), ("weights_x",), ("gains_x",), ("enc_x",), ("relay", 0, 0), ("enc_y",),
    ("enc_far",), ("arrive", 1, 0), ("arrive", 1, 1), ("own_head", 1), ("spread", 1, 0),
    ("feed_forward",), ("relay", 1, 0), ("weights_core",), ("other_head", 1), ("sum_yb",),
    ("sum_xa",), ("arrive", 2, 0), ("arrive", 2, 1), ("own_head", 2), ("spread", 2, 0),
    ("other_head", 0), ("other_head", 2), ("sum_z",), ("spread", 1, 1), ("relay", 2, 0),
    ("spread", 0, 1), ("spread", 2, 1), ("relay", 1, 1), ("relay", 0, 1), ("refine",),
    ("attend_to", 0, 3, 0, 3), ("relay", 2, 1), ("arrive", 3, 0), ("arrive", 3, 1),
    ("other_head", 3), ("own_head", 3), ("spread", 3, 0), ("refine_z",), ("attend_to", 3, 5, 0, 5),
    ("spread", 3, 1), ("attend_to", 5, 6, 0, 5), ("relay", 3, 0), ("attend_to", 0, 3, 3, 5),
    ("refine_all",), ("arrive", 4, 0), ("relay", 3, 1), ("arrive", 4, 1), ("own_head", 4),
    ("spread", 4, 0), ("other_head", 4), ("attend_to", 6, 7, 0, 5), ("modulate_x",),
    ("attend_to", 5, 7, 5, 7), ("spread", 4, 1), ("relay", 4, 0), ("attend_to", 7, 8, 0, 7),
    ("text",), ("relay", 4, 1), ("attend_to", 0, 5, 5, 7), ("attend_to", 0, 8, 7, 8, True),
    ("finish",),
)


def local(
    enc_states, image_count, prompt_count, enc_gain, enc_gate, enc_up, enc_down, final_gain, w_in,
    mod_text, mod_video, w_kv_text, w_qkv, query_gain, key_gain, text_key_gain, video_states,
):
    vmem, hbm = pl.BlockSpec(memory_space=pltpu.VMEM), pl.BlockSpec(memory_space=pl.ANY)
    smem = pl.BlockSpec(memory_space=pltpu.SMEM)
    row = lambda v: v.reshape(1, -1)
    return pl.pallas_call(
        block_kernel,
        out_shape=jax.ShapeDtypeStruct((128, 2048), BF16),
        in_specs=[smem] * 2 + [vmem] * 9 + [hbm] * 6,
        out_specs=vmem,
        scratch_shapes=[
            pltpu.VMEM((2, 8, 128, 128), BF16),
            pltpu.VMEM((4, 2, 8, 2, 128, 128), BF16),
            pltpu.VMEM((4, 2, 32, 128), BF16),
            pltpu.VMEM((8, 256, 256), F32),
            pltpu.VMEM((8, 256, 128), F32),
            pltpu.VMEM((16, 128, 128), BF16),
            pltpu.VMEM((128, D), BF16),
            pltpu.VMEM((256, D), BF16),
            pltpu.VMEM((256, D), BF16),
            pltpu.VMEM((256, D), BF16),
            pltpu.VMEM((128, D), BF16),
            pltpu.VMEM((2, D, 3 * HD), BF16),
            pltpu.VMEM((224, ED), BF16),
            pltpu.VMEM((224, ED), BF16),
            pltpu.VMEM((224, ED), BF16),
            pltpu.VMEM((2, 64, D), BF16),
            pltpu.VMEM((D, 2 * HD), BF16),
            pltpu.VMEM((8, 128, 128), BF16),
            pltpu.VMEM((8, 2, 128, 128), BF16),
            pltpu.VMEM((4, 2, 8, 16, 512), BF16),
            pltpu.VMEM((128, ED), BF16),
            pltpu.VMEM((128, ED), BF16),
            pltpu.VMEM((4, 128, 512), BF16),
            pltpu.VMEM((3, 128, 512), BF16),
            pltpu.VMEM((2, 4, 64, 512), BF16),
            pltpu.VMEM((4, 64, 512), BF16),
            pltpu.VMEM((2, 64, 512), F32),
            pltpu.VMEM((2, 64, 512), BF16),
            pltpu.VMEM((64, 512), BF16),
            pltpu.VMEM((4, 64, 512), BF16),
            pltpu.VMEM((3, 64, 512), BF16),
            pltpu.VMEM((8, 64, 128), BF16),
            pltpu.VMEM((7, 64, 128), BF16),
            pltpu.VMEM((2, 8, 128), F32),
            pltpu.VMEM((4, 16, D + 128), BF16),
            pltpu.VMEM((3, 16, D + 128), BF16),
            pltpu.VMEM((8, 16, 512), BF16),
            pltpu.VMEM((7, 16, 512), BF16),
            pltpu.VMEM((8, 16, 384), BF16),
            pltpu.VMEM((2, 16, D), BF16),
            pltpu.SemaphoreType.DMA((N_COPIES,)),
            pltpu.SemaphoreType.DMA((N_COPIES,)),
            pltpu.SemaphoreType.DMA((16,)),
            pltpu.SemaphoreType.DMA((16,)),
            pltpu.SemaphoreType.DMA((7,)),
        ],
        compiler_params=pltpu.CompilerParams(
            collective_id=0, has_side_effects=True, vmem_limit_bytes=58 * 2**20
        ),
        name="block",
    )(
        image_count, prompt_count, enc_states, video_states, mod_video[0], mod_text[0], row(enc_gain),
        row(final_gain), row(query_gain), row(key_gain), row(text_key_gain),
        w_qkv[:, 0, :], enc_gate.T, enc_up.T, enc_down, w_in, w_kv_text[:, 0, :],
    )


def solution(mesh):
    placed = (
        P(("grp", "blk", "head"), None),
        P("grp"),
        P("grp"),
        P(),
        P(None, ("blk", "head")),
        P(None, ("blk", "head")),
        P(("blk", "head"), None),
        P(("blk", "head")),
        P(("blk", "head"), None),
        P("grp", None, None),
        P("grp", None, None),
        P(None, "head", None),
        P(None, "head", None),
        P(),
        P(),
        P(),
        P(("grp", "blk", "head"), None),
    )
    return jax.shard_map(
        local,
        mesh=mesh,
        in_specs=placed,
        out_specs=P(("grp", "blk", "head"), None),
        check_vma=False,
    )
```

```python
import functools

import jax
import jax.numpy as jnp
from jax import lax
from jax.experimental import pallas as pl
from jax.experimental.pallas import tpu as pltpu
from jax.sharding import PartitionSpec as P

MESH = pl.DeviceIdType.MESH
EPS = 1e-06
NEG = -1e30
IMG_ROWS = 64
F32 = jnp.float32
BF16 = jnp.bfloat16
HD = 128
D = 3072
ED = 4096
STEP_CHUNKS = ((0, 1), (1, 2), (3, 2), (5, 2), (7, 1))
N_COPIES = 128


def dot(a, b):
    return jnp.dot(a, b, preferred_element_type=F32)


def dot_t(a, b):
    return lax.dot_general(a, b, (((1,), (1,)), ((), ())), preferred_element_type=F32)


def rms(values, gain):
    return values * lax.rsqrt(jnp.mean(values * values, axis=-1, keepdims=True) + EPS) * gain


class Links:
    def __init__(self, send, recv):
        self.send, self.recv, self.count, self.started = send, recv, 0, []

    def start(self, src, dst, device):
        copy = pltpu.make_async_remote_copy(
            src_ref=src,
            dst_ref=dst,
            send_sem=self.send.at[self.count],
            recv_sem=self.recv.at[self.count],
            device_id=device,
            device_id_type=MESH,
        )
        copy.start()
        self.count += 1
        assert self.count <= N_COPIES
        self.started.append(copy)
        return copy

    def drain(self):
        for copy in self.started:
            copy.wait_send()


def block_kernel(
    image_count, prompt_count,
    enc_own, video, mod_video, mod_text, enc_gain, final_gain, query_gain, key_gain, text_gain,
    w_qkv, gate_t, up_t, down, w_in, w_kv,
    out_ref,
    q_ref, kv_ref, text_ref, acc_ref, top_ref, staged,
    tok0, tok1, tok2, tok3, tok4, w_two, g_v, u_v, d_v, wi_v, wk_v,
    xq, xkv, granules, rows_v, normed_v, term_a, r_term_a, term_b, r_term_b, half_f, half_b,
    r_half, sum_b, r_sum_b, part, r_part,
    gain_v, proj, r_proj, proj_z, r_projz, cond, cond_mod,
    send, recv, out_send, out_recv, local_sem,
):
    g, y, h = lax.axis_index("grp"), lax.axis_index("blk"), lax.axis_index("head")
    z, X = h // 2, h % 2
    x_lo, core = g // 2, g % 2
    z_at = lambda dz: (g, y, ((z + dz) % 8) * 2 + X)
    y_at = lambda dy: (g, (y + dy) % 4, h)
    x_at = (g, y, z * 2 + (1 - X))
    w_at = ((g + 2) % 4, y, z * 2 + (1 - X))
    beside_at = ((g + 2) % 4, y, h)
    core_at = (g + 1 - 2 * core, y, h)

    def owner(k):
        c, x_rel = k % 8, k // 8
        offset = (c % 2) * (8 - (c + 1) // 2) + (1 - c % 2) * (c // 2)
        return (g, y, ((z + offset) % 8) * 2 + (X + x_rel) % 2)

    peers = [owner(k) for k in range(1, 16)] + [y_at(i) for i in range(1, 4)] + [w_at, beside_at, core_at]

    loads = [
        pltpu.make_async_copy(src, dst, local_sem.at[i])
        for i, (src, dst) in enumerate(
            [(w_qkv, w_two.at[0]), (gate_t, g_v), (up_t, u_v), (down, d_v), (w_in, wi_v.at[X]), (w_kv, wk_v)]
        )
    ]
    for load in loads:
        load.start()

    barrier = pltpu.get_barrier_semaphore()
    for peer in peers:
        pl.semaphore_signal(barrier, inc=1, device_id=peer, device_id_type=MESH)
    pl.semaphore_wait(barrier, len(peers))

    links = Links(send, recv)
    toks = [tok0, tok1, tok2, tok3, tok4]
    flight = {}

    def landed(name):
        for copy in flight[name]:
            copy.wait_recv()

    seen = set()

    def once(name):
        if name not in seen:
            seen.add(name)
            landed(name)

    def to_y(src, dst):
        return [links.start(src((y + i) % 4), dst(i), y_at(i)) for i in (1, 3, 2)]

    def to_z(src, dst):
        return [links.start(src((z + i) % 8), dst(i), z_at(i)) for i in (1, 7, 2, 6, 3, 5, 4)]

    def modulate_video(part):
        scale, shift = 1.0 + mod_video[1:2, :], mod_video[0:1, :]

        def modulate(i, _):
            at = pl.ds(pl.multiple_of(64 * part + i * 16, 16), 16)
            v = video[at, :].astype(F32)
            c = v - jnp.mean(v, axis=-1, keepdims=True)
            n = c * lax.rsqrt(jnp.mean(c * c, axis=-1, keepdims=True) + EPS)
            tok0[at, :] = (n * scale + shift).astype(BF16)
            return 0

        lax.fori_loop(0, 4, modulate, 0)

    def ring(step, part):
        at, low, high = pl.ds(64 * part, 64), 64 * part, 128 + 64 * part
        back = tok0.at[at] if step == 1 else toks[step - 1].at[pl.ds(high, 64)]
        copies = []
        if step < 4 or part == 0:
            copies.append(links.start(toks[step - 1].at[at], toks[step].at[at], z_at(1)))
        if step < 4:
            copies.append(links.start(back, toks[step].at[pl.ds(high, 64)], z_at(7)))
        elif part == 1:
            copies.append(links.start(back, tok4.at[at], z_at(7)))
        flight["tok", step, part] = copies

    def arrive(step, part):
        landed(("tok", step, part))
        if step < 4:
            ring(step + 1, part)

    def quarter(x_lo):
        return pl.ds(pl.multiple_of((2 * x_lo + core) * (D // 4), D // 4), D // 4)

    other = w_two.at[1]
    here, there = quarter(x_lo), quarter(1 - x_lo)

    def weights_x():
        flight["w_x"] = [links.start(w_qkv.at[there], other.at[there], w_at)]

    def weights_l():
        landed("w_x")
        flight["w_l"] = [
            links.start(other.at[here], other.at[here], beside_at),
            links.start(other.at[here], other.at[here], core_at),
        ]

    def weights_core():
        landed("w_l")
        flight["w_core"] = [links.start(other.at[there], other.at[there], core_at)]

    def project(step, which):
        first, count = STEP_CHUNKS[step]
        mixed = dot(toks[step][...], w_two[which])
        q = rms(mixed[:, :HD], query_gain[...]).astype(BF16)
        k = rms(mixed[:, HD : 2 * HD], key_gain[...]).astype(BF16)
        v = mixed[:, 2 * HD :].astype(BF16)
        for i in range(count):
            at = slice(i * 128, (i + 1) * 128)
            if which == 0:
                q_ref[0, first + i] = q[at]
                kv_ref[0, 0, first + i, 0] = k[at]
                kv_ref[0, 0, first + i, 1] = v[at]
            else:
                xq[first + i] = q[at]
                xkv[first + i, 0] = k[at]
                xkv[first + i, 1] = v[at]

    def spread(step, x_rel):
        chunks = pl.ds(*STEP_CHUNKS[step])
        if x_rel:
            landed(("x", step))
        mine = kv_ref.at[0, x_rel, chunks]
        flight["kv", step, x_rel] = [
            links.start(mine, kv_ref.at[3, x_rel, chunks], y_at(1)),
            links.start(mine, kv_ref.at[1, x_rel, chunks], y_at(3)),
        ]

    def relay(step, x_rel):
        chunks = pl.ds(*STEP_CHUNKS[step])
        landed(("kv", step, x_rel))
        far = kv_ref.at[2, x_rel, chunks]
        flight["far", step, x_rel] = [
            links.start(kv_ref.at[3, x_rel, chunks, 0], far.at[:, 0], y_at(1)),
            links.start(kv_ref.at[1, x_rel, chunks, 1], far.at[:, 1], y_at(3)),
        ]

    def own_head(step):
        if step == 0:
            loads[0].wait()
        project(step, 0)

    def other_head(step):
        once("w_core")
        chunks = pl.ds(*STEP_CHUNKS[step])
        project(step, 1)
        flight["q", step] = [links.start(xq.at[chunks], q_ref.at[1, chunks], x_at)]
        flight["x", step] = [links.start(xkv.at[chunks], kv_ref.at[0, 1, chunks], x_at)]

    def enc_z():
        rows = enc_own[...].astype(F32)
        pieces = [rows[:, 512 * j : 512 * j + 512] for j in range(8)]
        granules[y, X, z] = jnp.concatenate(pieces, axis=0).astype(BF16)
        flight["enc_z"] = to_z(lambda _: granules.at[y, X, z], lambda _: granules.at[y, X, z])

    def enc_x():
        landed("enc_z")
        flight["enc_x"] = [links.start(granules.at[y, X], granules.at[y, X], x_at)]

    def enc_y():
        landed("enc_x")
        mine = granules.at[y]
        flight["enc_y"] = [links.start(mine, mine, y_at(1)), links.start(mine, mine, y_at(3))]

    def enc_far():
        landed("enc_y")
        low, high = granules.at[(y + 3) % 4, 0], granules.at[(y + 1) % 4, 1]
        flight["enc_far"] = [links.start(low, low, y_at(1)), links.start(high, high, y_at(3))]

    w_in_half = pl.ds(pl.multiple_of(32 * core, 32), 32)

    def gains_x():
        gain = jnp.concatenate([final_gain[...], jnp.zeros((1, 64), F32)], axis=1)
        gain_v[X] = jnp.broadcast_to(gain, (8, 128))
        flight["gains"] = [
            links.start(gain_v.at[X], gain_v.at[X], x_at),
            links.start(w_in.at[w_in_half], wi_v.at[X, w_in_half], x_at),
        ]

    def gains_core():
        landed("gains")
        half = wi_v.at[1 - X, w_in_half]
        flight["gains_core"] = [links.start(half, half, core_at)]

    def feed_forward():
        landed("enc_far")
        out_at = lax.broadcasted_iota(jnp.int32, (256, 256), 0)
        in_at = lax.broadcasted_iota(jnp.int32, (256, 256), 1)
        source = out_at % 32 // 2 * 16 + out_at // 32 * 2 + out_at % 2
        order = (in_at == source).astype(F32).astype(BF16)
        for b in range(4):
            ordered = dot(order, granules[b].reshape(256, 512)).astype(BF16)
            for j in range(8):
                for x in (0, 1):
                    rows_v[64 * x + 16 * b : 64 * x + 16 * b + 16, 512 * j : 512 * j + 512] = ordered[
                        32 * j + 16 * x : 32 * j + 16 * x + 16
                    ]

        def normalize(i, _):
            at = pl.ds(pl.multiple_of(i * 16, 16), 16)
            v = rows_v[at, :].astype(F32)
            normed_v[at, :] = rms(v, enc_gain[...]).astype(BF16)
            return 0

        lax.fori_loop(0, 8, normalize, 0)
        loads[1].wait()
        loads[2].wait()
        gate = dot_t(normed_v[...], g_v[...])
        upward = dot_t(normed_v[...], u_v[...])
        hidden = (gate / (1.0 + jnp.exp(-gate)) * upward).astype(BF16)
        loads[3].wait()
        for b in range(4):
            product = dot(hidden, d_v[:, 1024 * b : 1024 * b + 1024]).astype(BF16)
            term_a[b] = product[:, :512]
            term_b[0, b] = product[:64, 512:]
            term_b[1, b] = product[64:, 512:]
        flight["sum_a"] = to_y(lambda b: term_a.at[b], lambda i: r_term_a.at[i - 1])
        flight["sum_b"] = [links.start(term_b.at[1 - X], r_term_b, x_at)]

    def sum_xa():
        landed("sum_a")
        total = term_a[y].astype(F32)
        for i in range(3):
            total = total + r_term_a[i].astype(F32)
        for x in (0, 1):
            half_f[x] = total[64 * x : 64 * x + 64]
            half_b[x] = total[64 * x : 64 * x + 64].astype(BF16)
        flight["sum_xa"] = [links.start(half_b.at[1 - X], r_half, x_at)]

    def sum_yb():
        landed("sum_b")
        for b in range(4):
            sum_b[b] = (term_b[X, b].astype(F32) + r_term_b[b].astype(F32)).astype(BF16)
        flight["sum_yb"] = to_y(lambda b: sum_b.at[b], lambda i: r_sum_b.at[i - 1])

    def sum_z():
        landed("sum_xa")
        landed("sum_yb")
        total = half_f[X] + r_half[...].astype(F32)
        for i in range(4):
            part[i] = total[:, 128 * i : 128 * i + 128].astype(BF16)
        total = sum_b[y].astype(F32)
        for i in range(3):
            total = total + r_sum_b[i].astype(F32)
        for i in range(4):
            part[4 + i] = total[:, 128 * i : 128 * i + 128].astype(BF16)
        flight["sum_z"] = to_z(lambda b: part.at[b], lambda i: r_part.at[i - 1])

    def refine():
        landed("sum_z")
        total = part[z].astype(F32)
        for i in range(7):
            total = total + r_part[i].astype(F32)
        column = pl.multiple_of(y * 1024 + z * 128, 128)
        own_rows = pl.ds(pl.multiple_of(X * 64, 64), 64)
        enc_out = total + rows_v[own_rows, pl.ds(column, 128)].astype(F32)
        squares = jnp.sum(enc_out * enc_out, axis=-1, keepdims=True)
        landed("gains_core")
        gain = jnp.concatenate([gain_v[0][:1, :64], gain_v[1][:1, :64]], axis=1)
        scaled = (enc_out * gain).astype(BF16)
        loads[4].wait()
        wide = jnp.broadcast_to(squares, (64, 128)).astype(BF16)
        for b in range(4):
            proj[b, :, D:] = wide[16 * b : 16 * b + 16]
        for i in range(6):
            weights = wi_v[:, :, 512 * i : 512 * i + 512].reshape(128, 512)
            product = dot(scaled, weights).astype(BF16)
            for b in range(4):
                proj[b, :, 512 * i : 512 * i + 512] = product[16 * b : 16 * b + 16]
        flight["ref_y"] = to_y(lambda b: proj.at[b], lambda i: r_proj.at[i - 1])

    def refine_z():
        landed("ref_y")
        total = proj[y].astype(F32)
        for i in range(3):
            total = total + r_proj[i].astype(F32)
        for i in range(8):
            proj_z[i, :, :384] = total[:, 384 * i : 384 * i + 384].astype(BF16)
            proj_z[i, :, 384:] = total[:, D:].astype(BF16)
        flight["ref_z"] = to_z(lambda b: proj_z.at[b], lambda i: r_projz.at[i - 1])

    def refine_all():
        landed("ref_z")
        total = proj_z[z].astype(F32)
        for i in range(7):
            total = total + r_projz[i].astype(F32)
        cond[z] = (total[:, :384] * lax.rsqrt(total[:, 384:385] / ED + EPS)).astype(BF16)
        flight["cond"] = to_z(lambda _: cond.at[z], lambda _: cond.at[z])

    def modulate_x():
        landed("cond")
        total = jnp.zeros((16, 1), F32)
        for i in range(8):
            total = total + jnp.sum(cond[i].astype(F32), axis=-1, keepdims=True)
        mean = total / D
        total = jnp.zeros((16, 1), F32)
        for i in range(8):
            c = cond[i].astype(F32) - mean
            total = total + jnp.sum(c * c, axis=-1, keepdims=True)
        inverse = lax.rsqrt(total / D + EPS)
        for i in range(8):
            at = slice(384 * i, 384 * i + 384)
            c = (cond[i].astype(F32) - mean) * inverse
            cond_mod[X, :, at] = (c * (1.0 + mod_text[1:2, at]) + mod_text[0:1, at]).astype(BF16)
        flight["cond_mod"] = [links.start(cond_mod.at[X], cond_mod.at[X], x_at)]

    def text():
        landed("cond_mod")
        loads[5].wait()
        text_kv = dot(cond_mod[...].reshape(32, D), wk_v[...])
        text_ref[y, 0] = rms(text_kv[:, :HD], text_gain[...]).astype(BF16)
        text_ref[y, 1] = text_kv[:, HD:].astype(BF16)
        flight["text"] = to_y(lambda _: text_ref.at[y], lambda _: text_ref.at[y])

    factor = HD ** (-0.5) * 1.4426950408889634

    def dead_bias():
        at = lax.broadcasted_iota(jnp.int32, (1, 128), 1)
        row = at // 32 * 32 + at // 2 % 8 * 4 + at // 16 % 2 * 2 + at % 2
        end = jnp.where(row < IMG_ROWS, image_count[0], IMG_ROWS + prompt_count[0])
        return jnp.where(row < end, 0.0, NEG)

    def attend(i, tiles, fresh, last):
        q = q_ref[:, i].reshape(256, 128)
        tiles = list(tiles) + (["text"] if last else [])

        def scores_of(n):
            if n == "text":
                return dot_t(q, text_ref[:, 0].reshape(128, 128)) * factor + dead_bias()
            return dot_t(q, kv_ref[:, :, n, 0].reshape(1024, 128)) * factor

        def values_of(n):
            if n == "text":
                v = text_ref[:, 1].reshape(128, 128)
            else:
                v = kv_ref[:, :, n, 1].reshape(1024, 128)
            return jnp.concatenate([v, jnp.ones(v.shape, BF16)], axis=1)

        highest = acc = None
        if not fresh:
            highest, acc = top_ref[i][:, :1], acc_ref[i]
        s = scores_of(tiles[0])
        for at, n in enumerate(tiles):
            following = scores_of(tiles[at + 1]) if at + 1 < len(tiles) else None
            top = jnp.max(s, axis=-1, keepdims=True)
            if highest is not None:
                top = jnp.maximum(highest, top)
            product = dot(jnp.exp2(s - top).astype(BF16), values_of(n))
            acc = product if highest is None else acc * jnp.exp2(highest - top) + product
            highest, s = top, following
        if not last:
            top_ref[i] = jnp.broadcast_to(highest, (256, 128))
            acc_ref[i] = acc
            return
        out = (acc[:, :HD] / acc[:, HD:]).astype(BF16)
        staged[i] = out[:128]
        staged[8 + i] = out[128:]
        deliver(8 + i).start()

        @pl.when(i > 0)
        def _():
            deliver(i).start()

    def queries(first, end, tiles, fresh, last=False):
        def body(i, _):
            attend(end - 1 - i, tiles, fresh, last)
            return 0

        lax.fori_loop(0, end - first, body, 0)

    def attend_to(first, end, key_first, key_end, last=False):
        for step, (chunk, _) in enumerate(STEP_CHUNKS):
            if chunk < key_end:
                once(("far", step, 0))
                once(("far", step, 1))
            if chunk < end:
                once(("q", step))
        if last:
            once("text")
        queries(first, end, range(key_first, key_end), key_first == 0, last)

    columns = pl.ds(pl.multiple_of(h * 128, 128), 128)

    def deliver(k):
        return pltpu.make_async_remote_copy(
            src_ref=staged.at[k],
            dst_ref=out_ref.at[:, columns],
            send_sem=out_send.at[k],
            recv_sem=out_recv.at[k],
            device_id=owner(k),
            device_id_type=MESH,
        )

    def finish():
        own = pltpu.make_async_copy(staged.at[0], out_ref.at[:, columns], local_sem.at[6])
        own.start()
        own.wait()
        links.drain()
        for k in range(1, 16):
            deliver(k).wait()

    stages = locals()
    for name, *step in PLAN:
        stages[name](*step)


PLAN = (
    ("enc_z",), ("modulate_video", 0), ("ring", 1, 0), ("modulate_video", 1), ("own_head", 0),
    ("ring", 1, 1), ("weights_x",), ("enc_x",), ("spread", 0, 0), ("enc_y",), ("arrive", 1, 0),
    ("weights_l",), ("enc_far",), ("arrive", 1, 1), ("own_head", 1), ("spread", 1, 0),
    ("relay", 1, 0), ("feed_forward",), ("weights_core",), ("arrive", 2, 0), ("other_head", 0),
    ("other_head", 1), ("arrive", 2, 1), ("own_head", 2), ("spread", 2, 0), ("sum_yb",),
    ("relay", 0, 0), ("other_head", 2), ("spread", 0, 1), ("spread", 1, 1), ("sum_xa",),
    ("gains_x",), ("spread", 2, 1), ("relay", 2, 0), ("relay", 0, 1), ("sum_z",), ("gains_core",),
    ("relay", 1, 1), ("arrive", 3, 0), ("arrive", 3, 1), ("own_head", 3), ("relay", 2, 1),
    ("other_head", 3), ("refine",), ("attend_to", 0, 3, 0, 3), ("spread", 3, 0),
    ("attend_to", 0, 3, 3, 5), ("refine_z",), ("arrive", 4, 0), ("spread", 3, 1), ("arrive", 4, 1),
    ("own_head", 4), ("spread", 4, 0), ("other_head", 4), ("attend_to", 6, 7, 0, 5),
    ("attend_to", 5, 6, 0, 5), ("relay", 3, 1), ("relay", 3, 0), ("refine_all",), ("relay", 4, 0),
    ("attend_to", 3, 5, 0, 5), ("modulate_x",), ("attend_to", 5, 7, 5, 7), ("spread", 4, 1),
    ("attend_to", 7, 8, 0, 7), ("text",), ("relay", 4, 1), ("attend_to", 0, 5, 5, 7),
    ("attend_to", 0, 8, 7, 8, True), ("finish",),
)


def local(
    enc_states, image_count, prompt_count, enc_gain, enc_gate, enc_up, enc_down, final_gain, w_in,
    mod_text, mod_video, w_kv_text, w_qkv, query_gain, key_gain, text_key_gain, video_states,
):
    vmem, hbm = pl.BlockSpec(memory_space=pltpu.VMEM), pl.BlockSpec(memory_space=pl.ANY)
    smem = pl.BlockSpec(memory_space=pltpu.SMEM)
    row = lambda v: v.reshape(1, -1)
    return pl.pallas_call(
        block_kernel,
        out_shape=jax.ShapeDtypeStruct((128, 2048), BF16),
        in_specs=[smem] * 2 + [vmem] * 9 + [hbm] * 6,
        out_specs=vmem,
        scratch_shapes=[
            pltpu.VMEM((2, 8, 128, 128), BF16),
            pltpu.VMEM((4, 2, 8, 2, 128, 128), BF16),
            pltpu.VMEM((4, 2, 32, 128), BF16),
            pltpu.VMEM((8, 256, 256), F32),
            pltpu.VMEM((8, 256, 128), F32),
            pltpu.VMEM((16, 128, 128), BF16),
            pltpu.VMEM((128, D), BF16),
            pltpu.VMEM((256, D), BF16),
            pltpu.VMEM((256, D), BF16),
            pltpu.VMEM((256, D), BF16),
            pltpu.VMEM((128, D), BF16),
            pltpu.VMEM((2, D, 3 * HD), BF16),
            pltpu.VMEM((224, ED), BF16),
            pltpu.VMEM((224, ED), BF16),
            pltpu.VMEM((224, ED), BF16),
            pltpu.VMEM((2, 64, D), BF16),
            pltpu.VMEM((D, 2 * HD), BF16),
            pltpu.VMEM((8, 128, 128), BF16),
            pltpu.VMEM((8, 2, 128, 128), BF16),
            pltpu.VMEM((4, 2, 8, 16, 512), BF16),
            pltpu.VMEM((128, ED), BF16),
            pltpu.VMEM((128, ED), BF16),
            pltpu.VMEM((4, 128, 512), BF16),
            pltpu.VMEM((3, 128, 512), BF16),
            pltpu.VMEM((2, 4, 64, 512), BF16),
            pltpu.VMEM((4, 64, 512), BF16),
            pltpu.VMEM((2, 64, 512), F32),
            pltpu.VMEM((2, 64, 512), BF16),
            pltpu.VMEM((64, 512), BF16),
            pltpu.VMEM((4, 64, 512), BF16),
            pltpu.VMEM((3, 64, 512), BF16),
            pltpu.VMEM((8, 64, 128), BF16),
            pltpu.VMEM((7, 64, 128), BF16),
            pltpu.VMEM((2, 8, 128), F32),
            pltpu.VMEM((4, 16, D + 128), BF16),
            pltpu.VMEM((3, 16, D + 128), BF16),
            pltpu.VMEM((8, 16, 512), BF16),
            pltpu.VMEM((7, 16, 512), BF16),
            pltpu.VMEM((8, 16, 384), BF16),
            pltpu.VMEM((2, 16, D), BF16),
            pltpu.SemaphoreType.DMA((N_COPIES,)),
            pltpu.SemaphoreType.DMA((N_COPIES,)),
            pltpu.SemaphoreType.DMA((16,)),
            pltpu.SemaphoreType.DMA((16,)),
            pltpu.SemaphoreType.DMA((7,)),
        ],
        compiler_params=pltpu.CompilerParams(
            collective_id=0, has_side_effects=True, vmem_limit_bytes=58 * 2**20
        ),
        name="block",
    )(
        image_count, prompt_count, enc_states, video_states, mod_video[0], mod_text[0], row(enc_gain),
        row(final_gain), row(query_gain), row(key_gain), row(text_key_gain),
        w_qkv[:, 0, :], enc_gate.T, enc_up.T, enc_down, w_in, w_kv_text[:, 0, :],
    )


def solution(mesh):
    placed = (
        P(("grp", "blk", "head"), None),
        P("grp"),
        P("grp"),
        P(),
        P(None, ("blk", "head")),
        P(None, ("blk", "head")),
        P(("blk", "head"), None),
        P(("blk", "head")),
        P(("blk", "head"), None),
        P("grp", None, None),
        P("grp", None, None),
        P(None, "head", None),
        P(None, "head", None),
        P(),
        P(),
        P(),
        P(("grp", "blk", "head"), None),
    )
    return jax.shard_map(
        local,
        mesh=mesh,
        in_specs=placed,
        out_specs=P(("grp", "blk", "head"), None),
        check_vma=False,
    )
```

```python
import functools

import jax
import jax.numpy as jnp
from jax import lax
from jax.experimental import pallas as pl
from jax.experimental.pallas import tpu as pltpu
from jax.sharding import PartitionSpec as P

MESH = pl.DeviceIdType.MESH
EPS = 1e-06
NEG = -1e30
IMG_ROWS = 64
F32 = jnp.float32
BF16 = jnp.bfloat16
HD = 128
D = 3072
ED = 4096
STEP_CHUNKS = ((0, 1), (1, 2), (3, 2), (5, 2), (7, 1))
N_COPIES = 128
DIRECT = (3, 4)


def dot(a, b):
    return jnp.dot(a, b, preferred_element_type=F32)


def dot_t(a, b):
    return lax.dot_general(a, b, (((1,), (1,)), ((), ())), preferred_element_type=F32)


def rms(values, gain):
    return values * lax.rsqrt(jnp.mean(values * values, axis=-1, keepdims=True) + EPS) * gain


class Links:
    def __init__(self, send, recv):
        self.send, self.recv, self.count, self.started = send, recv, 0, []

    def start(self, src, dst, device):
        copy = pltpu.make_async_remote_copy(
            src_ref=src,
            dst_ref=dst,
            send_sem=self.send.at[self.count],
            recv_sem=self.recv.at[self.count],
            device_id=device,
            device_id_type=MESH,
        )
        copy.start()
        self.count += 1
        assert self.count <= N_COPIES
        self.started.append(copy)
        return copy

    def drain(self, keep=0):
        while len(self.started) > keep:
            self.started.pop(0).wait_send()


def block_kernel(
    image_count, prompt_count,
    enc_own, mod_video, mod_text, enc_gain, final_gain, query_gain, key_gain, text_gain,
    video, w_qkv, gate_t, up_t, down, w_in, w_kv,
    out_ref,
    video_v, q_ref, kv_ref, text_ref, acc_ref, top_ref, staged,
    tok0, tok1, tok2, tok3, tok4, w_two, g_v, u_v, d_v, wi_v, wk_v,
    xq, xkv, granules, rows_v, normed_v, term_a, r_term_a, term_b, r_term_b, half_f, half_b,
    r_half, sum_b, r_sum_b, part, r_part,
    gain_v, proj, r_proj, proj_z, r_projz, cond, cond_mod,
    send, recv, out_send, out_recv, local_sem,
):
    g, y, h = lax.axis_index("grp"), lax.axis_index("blk"), lax.axis_index("head")
    z, X = h // 2, h % 2
    core = g % 2
    z_at = lambda dz: (g, y, ((z + dz) % 8) * 2 + X)
    y_at = lambda dy: (g, (y + dy) % 4, h)
    x_at = (g, y, z * 2 + (1 - X))
    w_at = ((g + 2) % 4, y, z * 2 + (1 - X))
    core_at = (g + 1 - 2 * core, y, h)

    def owner(k):
        c, x_rel = k % 8, k // 8
        offset = (c % 2) * (8 - (c + 1) // 2) + (1 - c % 2) * (c // 2)
        return (g, y, ((z + offset) % 8) * 2 + (X + x_rel) % 2)

    peers = [owner(k) for k in range(1, 16)] + [y_at(i) for i in range(1, 4)] + [w_at, core_at]

    loads = [
        pltpu.make_async_copy(src, dst, local_sem.at[i])
        for i, (src, dst) in enumerate(
            [(video, video_v), (w_qkv, w_two.at[0]), (gate_t, g_v), (up_t, u_v), (down, d_v), (w_in, wi_v.at[X]), (w_kv, wk_v)]
        )
    ]
    for load in loads:
        load.start()

    barrier = pltpu.get_barrier_semaphore()
    for peer in peers:
        pl.semaphore_signal(barrier, inc=1, device_id=peer, device_id_type=MESH)
    pl.semaphore_wait(barrier, len(peers))

    links = Links(send, recv)
    toks = [tok0, tok1, tok2, tok3, tok4]
    flight = {}

    def landed(name):
        for copy in flight[name]:
            copy.wait_recv()

    seen = set()

    def once(name):
        if name not in seen:
            seen.add(name)
            landed(name)

    def to_y(src, dst):
        return [links.start(src((y + i) % 4), dst(i), y_at(i)) for i in (1, 3, 2)]

    def to_sides(block):
        return [links.start(block, block, y_at(1)), links.start(block, block, y_at(3))]

    def to_z(src, dst):
        return [links.start(src((z + i) % 8), dst(i), z_at(i)) for i in (1, 7, 2, 6, 3, 5, 4)]

    def modulate_video(part):
        if part == 0:
            loads[0].wait()
        scale, shift = 1.0 + mod_video[1:2, :], mod_video[0:1, :]

        def modulate(i, _):
            at = pl.ds(pl.multiple_of(64 * part + i * 16, 16), 16)
            v = video_v[at, :].astype(F32)
            c = v - jnp.mean(v, axis=-1, keepdims=True)
            n = c * lax.rsqrt(jnp.mean(c * c, axis=-1, keepdims=True) + EPS)
            tok0[at, :] = (n * scale + shift).astype(BF16)
            return 0

        lax.fori_loop(0, 4, modulate, 0)

    def ring(step, part):
        at, low, high = pl.ds(64 * part, 64), 64 * part, 128 + 64 * part
        back = tok0.at[at] if step == 1 else toks[step - 1].at[pl.ds(high, 64)]
        copies = []
        if step < 4 or part == 0:
            copies.append(links.start(toks[step - 1].at[at], toks[step].at[at], z_at(1)))
        if step < 4:
            copies.append(links.start(back, toks[step].at[pl.ds(high, 64)], z_at(7)))
        elif part == 1:
            copies.append(links.start(back, tok4.at[at], z_at(7)))
        flight["tok", step, part] = copies

    def arrive(step, part):
        landed(("tok", step, part))
        if step < 4:
            ring(step + 1, part)

    other = w_two.at[1]

    def eighth(block, start=0, count=D // 8):
        first = (2 * block + core) * (D // 8) + start
        return other.at[pl.ds(pl.multiple_of(first, D // 16), count)]

    def to_core(*parts):
        return [links.start(part, part, core_at) for part in parts]

    def weights_x():
        mine = pl.ds(pl.multiple_of((2 * y + core) * (D // 8), D // 8), D // 8)
        flight["w_x"] = [links.start(w_qkv.at[mine], other.at[mine], w_at)]

    def weights_y():
        landed("w_x")
        flight["w_y"] = to_sides(eighth(y))
        flight["w_core"] = to_core(eighth(y))

    def weights_far():
        landed("w_y")
        below, above = (y + 3) % 4, (y + 1) % 4
        low, high = eighth(below, 0, D // 16), eighth(above, D // 16, D // 16)
        flight["w_far"] = [links.start(low, low, y_at(1)), links.start(high, high, y_at(3))]
        flight["w_core"] += to_core(eighth(below), eighth(above))

    def weights_core():
        landed("w_far")
        flight["w_core"] += to_core(eighth((y + 2) % 4))

    def project(step, which):
        first, count = STEP_CHUNKS[step]
        mixed = dot(toks[step][...], w_two[which])
        q = rms(mixed[:, :HD], query_gain[...]).astype(BF16)
        k = rms(mixed[:, HD : 2 * HD], key_gain[...]).astype(BF16)
        v = mixed[:, 2 * HD :].astype(BF16)
        for i in range(count):
            at = slice(i * 128, (i + 1) * 128)
            if which == 0:
                q_ref[0, first + i] = q[at]
                kv_ref[0, 0, first + i, 0] = k[at]
                kv_ref[0, 0, first + i, 1] = v[at]
            else:
                xq[first + i] = q[at]
                xkv[first + i, 0] = k[at]
                xkv[first + i, 1] = v[at]

    def spread(step, x_rel):
        chunks = pl.ds(*STEP_CHUNKS[step])
        if x_rel:
            landed(("x", step))
        mine = kv_ref.at[0, x_rel, chunks]
        flight["kv", step, x_rel] = [
            links.start(mine, kv_ref.at[3, x_rel, chunks], y_at(1)),
            links.start(mine, kv_ref.at[1, x_rel, chunks], y_at(3)),
        ]
        if step in DIRECT:
            last = links.start(mine, kv_ref.at[2, x_rel, chunks], y_at(2))
            flight["far", step, x_rel] = flight["kv", step, x_rel] + [last]

    def relay(step, x_rel):
        chunks = pl.ds(*STEP_CHUNKS[step])
        landed(("kv", step, x_rel))
        far = kv_ref.at[2, x_rel, chunks]
        flight["far", step, x_rel] = [
            links.start(kv_ref.at[3, x_rel, chunks, 0], far.at[:, 0], y_at(1)),
            links.start(kv_ref.at[1, x_rel, chunks, 1], far.at[:, 1], y_at(3)),
        ]

    def own_head(step):
        if step == 0:
            loads[1].wait()
        project(step, 0)

    def other_head(step):
        once("w_core")
        chunks = pl.ds(*STEP_CHUNKS[step])
        project(step, 1)
        flight["q", step] = [links.start(xq.at[chunks], q_ref.at[1, chunks], x_at)]
        flight["x", step] = [links.start(xkv.at[chunks], kv_ref.at[0, 1, chunks], x_at)]

    def enc_z():
        rows = enc_own[...].astype(F32)
        pieces = [rows[:, 512 * j : 512 * j + 512] for j in range(8)]
        granules[y, X, z] = jnp.concatenate(pieces, axis=0).astype(BF16)
        flight["enc_z"] = to_z(lambda _: granules.at[y, X, z], lambda _: granules.at[y, X, z])

    def enc_x():
        landed("enc_z")
        flight["enc_x"] = [links.start(granules.at[y, X], granules.at[y, X], x_at)]

    def enc_y():
        landed("enc_x")
        mine = granules.at[y]
        flight["enc_y"] = [links.start(mine, mine, y_at(1)), links.start(mine, mine, y_at(3))]

    def enc_far():
        landed("enc_y")
        low, high = granules.at[(y + 3) % 4, 0], granules.at[(y + 1) % 4, 1]
        flight["enc_far"] = [links.start(low, low, y_at(1)), links.start(high, high, y_at(3))]

    w_in_half = pl.ds(pl.multiple_of(32 * core, 32), 32)

    def gains_x():
        gain = jnp.concatenate([final_gain[...], jnp.zeros((1, 64), F32)], axis=1)
        gain_v[X] = jnp.broadcast_to(gain, (8, 128))
        flight["gains"] = [
            links.start(gain_v.at[X], gain_v.at[X], x_at),
            links.start(w_in.at[w_in_half], wi_v.at[X, w_in_half], x_at),
        ]

    def gains_core():
        landed("gains")
        half = wi_v.at[1 - X, w_in_half]
        flight["gains_core"] = [links.start(half, half, core_at)]

    def feed_forward():
        landed("enc_far")
        out_at = lax.broadcasted_iota(jnp.int32, (256, 256), 0)
        in_at = lax.broadcasted_iota(jnp.int32, (256, 256), 1)
        source = out_at % 32 // 2 * 16 + out_at // 32 * 2 + out_at % 2
        order = (in_at == source).astype(F32).astype(BF16)
        for b in range(4):
            ordered = dot(order, granules[b].reshape(256, 512)).astype(BF16)
            for j in range(8):
                for x in (0, 1):
                    rows_v[64 * x + 16 * b : 64 * x + 16 * b + 16, 512 * j : 512 * j + 512] = ordered[
                        32 * j + 16 * x : 32 * j + 16 * x + 16
                    ]

        def normalize(i, _):
            at = pl.ds(pl.multiple_of(i * 16, 16), 16)
            v = rows_v[at, :].astype(F32)
            normed_v[at, :] = rms(v, enc_gain[...]).astype(BF16)
            return 0

        lax.fori_loop(0, 8, normalize, 0)
        loads[2].wait()
        loads[3].wait()
        gate = dot_t(normed_v[...], g_v[...])
        upward = dot_t(normed_v[...], u_v[...])
        hidden = (gate / (1.0 + jnp.exp(-gate)) * upward).astype(BF16)
        loads[4].wait()
        for b in range(4):
            product = dot(hidden, d_v[:, 1024 * b : 1024 * b + 1024]).astype(BF16)
            term_a[b] = product[:, :512]
            term_b[0, b] = product[:64, 512:]
            term_b[1, b] = product[64:, 512:]
        flight["sum_a"] = to_y(lambda b: term_a.at[b], lambda i: r_term_a.at[i - 1])
        flight["sum_b"] = [links.start(term_b.at[1 - X], r_term_b, x_at)]

    def sum_xa():
        landed("sum_a")
        total = term_a[y].astype(F32)
        for i in range(3):
            total = total + r_term_a[i].astype(F32)
        for x in (0, 1):
            half_f[x] = total[64 * x : 64 * x + 64]
            half_b[x] = total[64 * x : 64 * x + 64].astype(BF16)
        flight["sum_xa"] = [links.start(half_b.at[1 - X], r_half, x_at)]

    def sum_yb():
        landed("sum_b")
        for b in range(4):
            sum_b[b] = (term_b[X, b].astype(F32) + r_term_b[b].astype(F32)).astype(BF16)
        flight["sum_yb"] = to_y(lambda b: sum_b.at[b], lambda i: r_sum_b.at[i - 1])

    def sum_z():
        landed("sum_xa")
        landed("sum_yb")
        total = half_f[X] + r_half[...].astype(F32)
        for i in range(4):
            part[i] = total[:, 128 * i : 128 * i + 128].astype(BF16)
        total = sum_b[y].astype(F32)
        for i in range(3):
            total = total + r_sum_b[i].astype(F32)
        for i in range(4):
            part[4 + i] = total[:, 128 * i : 128 * i + 128].astype(BF16)
        flight["sum_z"] = to_z(lambda b: part.at[b], lambda i: r_part.at[i - 1])

    def refine():
        landed("sum_z")
        total = part[z].astype(F32)
        for i in range(7):
            total = total + r_part[i].astype(F32)
        column = pl.multiple_of(y * 1024 + z * 128, 128)
        own_rows = pl.ds(pl.multiple_of(X * 64, 64), 64)
        enc_out = total + rows_v[own_rows, pl.ds(column, 128)].astype(F32)
        squares = jnp.sum(enc_out * enc_out, axis=-1, keepdims=True)
        landed("gains_core")
        gain = jnp.concatenate([gain_v[0][:1, :64], gain_v[1][:1, :64]], axis=1)
        scaled = (enc_out * gain).astype(BF16)
        loads[5].wait()
        wide = jnp.broadcast_to(squares, (64, 128)).astype(BF16)
        for b in range(4):
            proj[b, :, D:] = wide[16 * b : 16 * b + 16]
        for i in range(6):
            weights = wi_v[:, :, 512 * i : 512 * i + 512].reshape(128, 512)
            product = dot(scaled, weights).astype(BF16)
            for b in range(4):
                proj[b, :, 512 * i : 512 * i + 512] = product[16 * b : 16 * b + 16]
        flight["ref_y"] = to_y(lambda b: proj.at[b], lambda i: r_proj.at[i - 1])

    def refine_z():
        landed("ref_y")
        total = proj[y].astype(F32)
        for i in range(3):
            total = total + r_proj[i].astype(F32)
        for i in range(8):
            proj_z[i, :, :384] = total[:, 384 * i : 384 * i + 384].astype(BF16)
            proj_z[i, :, 384:] = total[:, D:].astype(BF16)
        flight["ref_z"] = to_z(lambda b: proj_z.at[b], lambda i: r_projz.at[i - 1])

    def refine_all():
        landed("ref_z")
        total = proj_z[z].astype(F32)
        for i in range(7):
            total = total + r_projz[i].astype(F32)
        cond[z] = (total[:, :384] * lax.rsqrt(total[:, 384:385] / ED + EPS)).astype(BF16)
        flight["cond"] = to_z(lambda _: cond.at[z], lambda _: cond.at[z])

    def modulate_x():
        landed("cond")
        total = jnp.zeros((16, 1), F32)
        for i in range(8):
            total = total + jnp.sum(cond[i].astype(F32), axis=-1, keepdims=True)
        mean = total / D
        total = jnp.zeros((16, 1), F32)
        for i in range(8):
            c = cond[i].astype(F32) - mean
            total = total + jnp.sum(c * c, axis=-1, keepdims=True)
        inverse = lax.rsqrt(total / D + EPS)
        for i in range(8):
            at = slice(384 * i, 384 * i + 384)
            c = (cond[i].astype(F32) - mean) * inverse
            cond_mod[X, :, at] = (c * (1.0 + mod_text[1:2, at]) + mod_text[0:1, at]).astype(BF16)
        flight["cond_mod"] = [links.start(cond_mod.at[X], cond_mod.at[X], x_at)]

    def text():
        landed("cond_mod")
        loads[6].wait()
        text_kv = dot(cond_mod[...].reshape(32, D), wk_v[...])
        text_ref[y, 0] = rms(text_kv[:, :HD], text_gain[...]).astype(BF16)
        text_ref[y, 1] = text_kv[:, HD:].astype(BF16)
        flight["text"] = to_y(lambda _: text_ref.at[y], lambda _: text_ref.at[y])

    factor = HD ** (-0.5) * 1.4426950408889634

    def dead_bias():
        at = lax.broadcasted_iota(jnp.int32, (1, 128), 1)
        row = at // 32 * 32 + at // 2 % 8 * 4 + at // 16 % 2 * 2 + at % 2
        end = jnp.where(row < IMG_ROWS, image_count[0], IMG_ROWS + prompt_count[0])
        return jnp.where(row < end, 0.0, NEG)

    def attend(group, tiles, fresh, last):
        tiles = list(tiles) + (["text"] if last else [])
        items = [(i, n) for i in range(len(group)) for n in tiles]

        def scores_of(item):
            i, n = item
            q = q_ref[:, group[i]].reshape(256, 128)
            if n == "text":
                return dot_t(q, text_ref[:, 0].reshape(128, 128)) * factor + dead_bias()
            return dot_t(q, kv_ref[:, :, n, 0].reshape(1024, 128)) * factor

        def values_of(n):
            if n == "text":
                v = text_ref[:, 1].reshape(128, 128)
            else:
                v = kv_ref[:, :, n, 1].reshape(1024, 128)
            return jnp.concatenate([v, jnp.ones(v.shape, BF16)], axis=1)

        s = scores_of(items[0])
        for at, (i, n) in enumerate(items):
            chunk = group[i]
            if n == tiles[0]:
                highest = acc = None
                if not fresh:
                    highest, acc = top_ref[chunk][:, :1], acc_ref[chunk]
            following = scores_of(items[at + 1]) if at + 1 < len(items) else None
            top = jnp.max(s, axis=-1, keepdims=True)
            if highest is not None:
                top = jnp.maximum(highest, top)
            product = dot(jnp.exp2(s - top).astype(BF16), values_of(n))
            acc = product if highest is None else acc * jnp.exp2(highest - top) + product
            highest, s = top, following
            if n == tiles[-1]:
                if last:
                    send_out(chunk, (acc[:, :HD] / acc[:, HD:]).astype(BF16))
                else:
                    top_ref[chunk] = jnp.broadcast_to(highest, (256, 128))
                    acc_ref[chunk] = acc

    def send_out(chunk, out):
        staged[chunk] = out[:128]
        staged[8 + chunk] = out[128:]
        deliver(8 + chunk).start()

        @pl.when(chunk > 0)
        def _():
            deliver(chunk).start()

    def queries(first, end, tiles, fresh, last=False):
        count = end - first
        size = 4 if last else count

        def body(turn, _):
            attend([end - 1 - (turn * size + k) for k in range(size)], tiles, fresh, last)
            return 0

        if size == count:
            body(0, 0)
        else:
            lax.fori_loop(0, count // size, body, 0)

    def attend_to(first, end, key_first, key_end, last=False):
        for step, (chunk, _) in enumerate(STEP_CHUNKS):
            if chunk < key_end:
                once(("far", step, 0))
                once(("far", step, 1))
            if chunk < end:
                once(("q", step))
        if last:
            once("text")
        queries(first, end, range(key_first, key_end), key_first == 0, last)

    columns = pl.ds(pl.multiple_of(h * 128, 128), 128)

    def deliver(k):
        return pltpu.make_async_remote_copy(
            src_ref=staged.at[k],
            dst_ref=out_ref.at[:, columns],
            send_sem=out_send.at[k],
            recv_sem=out_recv.at[k],
            device_id=owner(k),
            device_id_type=MESH,
        )

    def drain():
        links.drain(24)

    def finish():
        own = pltpu.make_async_copy(staged.at[0], out_ref.at[:, columns], local_sem.at[7])
        own.start()
        own.wait()
        links.drain()
        for k in range(1, 16):
            deliver(k).wait()

    stages = locals()
    for name, *step in PLAN:
        stages[name](*step)


PLAN = (
    ("enc_z",), ("modulate_video", 0), ("ring", 1, 0), ("enc_x",), ("modulate_video", 1),
    ("ring", 1, 1), ("own_head", 0), ("spread", 0, 0), ("weights_x",), ("enc_y",), ("weights_y",),
    ("arrive", 1, 0), ("enc_far",), ("arrive", 1, 1), ("weights_far",), ("feed_forward",),
    ("own_head", 1), ("arrive", 2, 0), ("spread", 1, 0), ("weights_core",), ("other_head", 0),
    ("other_head", 1), ("relay", 0, 0), ("arrive", 2, 1), ("sum_yb",), ("other_head", 2),
    ("own_head", 2), ("spread", 2, 0), ("spread", 0, 1), ("spread", 1, 1), ("sum_xa",),
    ("gains_x",), ("spread", 2, 1), ("sum_z",), ("relay", 1, 0), ("relay", 1, 1), ("gains_core",),
    ("relay", 0, 1), ("drain",), ("arrive", 3, 0), ("arrive", 3, 1), ("other_head", 3),
    ("relay", 2, 1), ("own_head", 3), ("relay", 2, 0), ("refine",), ("attend_to", 0, 3, 0, 3),
    ("spread", 3, 0), ("attend_to", 3, 5, 0, 5), ("spread", 3, 1), ("refine_z",), ("drain",),
    ("arrive", 4, 0), ("attend_to", 5, 6, 0, 5), ("attend_to", 6, 7, 0, 5), ("arrive", 4, 1),
    ("refine_all",), ("other_head", 4), ("own_head", 4), ("attend_to", 0, 3, 3, 5),
    ("spread", 4, 0), ("modulate_x",), ("attend_to", 5, 7, 5, 7), ("spread", 4, 1),
    ("attend_to", 7, 8, 0, 7), ("text",), ("attend_to", 0, 5, 5, 7), ("drain",),
    ("attend_to", 0, 8, 7, 8, True), ("finish",),
)


def local(
    enc_states, image_count, prompt_count, enc_gain, enc_gate, enc_up, enc_down, final_gain, w_in,
    mod_text, mod_video, w_kv_text, w_qkv, query_gain, key_gain, text_key_gain, video_states,
):
    vmem, hbm = pl.BlockSpec(memory_space=pltpu.VMEM), pl.BlockSpec(memory_space=pl.ANY)
    smem = pl.BlockSpec(memory_space=pltpu.SMEM)
    row = lambda v: v.reshape(1, -1)
    return pl.pallas_call(
        block_kernel,
        out_shape=jax.ShapeDtypeStruct((128, 2048), BF16),
        in_specs=[smem] * 2 + [vmem] * 8 + [hbm] * 7,
        out_specs=hbm,
        scratch_shapes=[
            pltpu.VMEM((128, D), BF16),
            pltpu.VMEM((2, 8, 128, 128), BF16),
            pltpu.VMEM((4, 2, 8, 2, 128, 128), BF16),
            pltpu.VMEM((4, 2, 32, 128), BF16),
            pltpu.VMEM((8, 256, 256), F32),
            pltpu.VMEM((8, 256, 128), F32),
            pltpu.VMEM((16, 128, 128), BF16),
            pltpu.VMEM((128, D), BF16),
            pltpu.VMEM((256, D), BF16),
            pltpu.VMEM((256, D), BF16),
            pltpu.VMEM((256, D), BF16),
            pltpu.VMEM((128, D), BF16),
            pltpu.VMEM((2, D, 3 * HD), BF16),
            pltpu.VMEM((224, ED), BF16),
            pltpu.VMEM((224, ED), BF16),
            pltpu.VMEM((224, ED), BF16),
            pltpu.VMEM((2, 64, D), BF16),
            pltpu.VMEM((D, 2 * HD), BF16),
            pltpu.VMEM((8, 128, 128), BF16),
            pltpu.VMEM((8, 2, 128, 128), BF16),
            pltpu.VMEM((4, 2, 8, 16, 512), BF16),
            pltpu.VMEM((128, ED), BF16),
            pltpu.VMEM((128, ED), BF16),
            pltpu.VMEM((4, 128, 512), BF16),
            pltpu.VMEM((3, 128, 512), BF16),
            pltpu.VMEM((2, 4, 64, 512), BF16),
            pltpu.VMEM((4, 64, 512), BF16),
            pltpu.VMEM((2, 64, 512), F32),
            pltpu.VMEM((2, 64, 512), BF16),
            pltpu.VMEM((64, 512), BF16),
            pltpu.VMEM((4, 64, 512), BF16),
            pltpu.VMEM((3, 64, 512), BF16),
            pltpu.VMEM((8, 64, 128), BF16),
            pltpu.VMEM((7, 64, 128), BF16),
            pltpu.VMEM((2, 8, 128), F32),
            pltpu.VMEM((4, 16, D + 128), BF16),
            pltpu.VMEM((3, 16, D + 128), BF16),
            pltpu.VMEM((8, 16, 512), BF16),
            pltpu.VMEM((7, 16, 512), BF16),
            pltpu.VMEM((8, 16, 384), BF16),
            pltpu.VMEM((2, 16, D), BF16),
            pltpu.SemaphoreType.DMA((N_COPIES,)),
            pltpu.SemaphoreType.DMA((N_COPIES,)),
            pltpu.SemaphoreType.DMA((16,)),
            pltpu.SemaphoreType.DMA((16,)),
            pltpu.SemaphoreType.DMA((8,)),
        ],
        compiler_params=pltpu.CompilerParams(
            collective_id=0, has_side_effects=True, vmem_limit_bytes=58 * 2**20
        ),
        name="block",
    )(
        image_count, prompt_count, enc_states, mod_video[0], mod_text[0], row(enc_gain),
        row(final_gain), row(query_gain), row(key_gain), row(text_key_gain),
        video_states, w_qkv[:, 0, :], enc_gate.T, enc_up.T, enc_down, w_in, w_kv_text[:, 0, :],
    )


def solution(mesh):
    placed = (
        P(("grp", "blk", "head"), None),
        P("grp"),
        P("grp"),
        P(),
        P(None, ("blk", "head")),
        P(None, ("blk", "head")),
        P(("blk", "head"), None),
        P(("blk", "head")),
        P(("blk", "head"), None),
        P("grp", None, None),
        P("grp", None, None),
        P(None, "head", None),
        P(None, "head", None),
        P(),
        P(),
        P(),
        P(("grp", "blk", "head"), None),
    )
    return jax.shard_map(
        local,
        mesh=mesh,
        in_specs=placed,
        out_specs=P(("grp", "blk", "head"), None),
        check_vma=False,
    )
```

```python
import functools

import jax
import jax.numpy as jnp
from jax import lax
from jax.experimental import pallas as pl
from jax.experimental.pallas import tpu as pltpu
from jax.sharding import PartitionSpec as P

MESH = pl.DeviceIdType.MESH
EPS = 1e-06
NEG = -1e30
IMG_ROWS = 64
F32 = jnp.float32
BF16 = jnp.bfloat16
HD = 128
D = 3072
ED = 4096
STEP_CHUNKS = ((0, 1), (1, 2), (3, 2), (5, 2), (7, 1))
N_COPIES = 128
DIRECT = (3, 4)


def dot(a, b):
    return jnp.dot(a, b, preferred_element_type=F32)


def dot_t(a, b):
    return lax.dot_general(a, b, (((1,), (1,)), ((), ())), preferred_element_type=F32)


def rms(values, gain):
    return values * lax.rsqrt(jnp.mean(values * values, axis=-1, keepdims=True) + EPS) * gain


class Links:
    def __init__(self, send, recv):
        self.send, self.recv, self.count, self.started = send, recv, 0, []

    def start(self, src, dst, device):
        copy = pltpu.make_async_remote_copy(
            src_ref=src,
            dst_ref=dst,
            send_sem=self.send.at[self.count],
            recv_sem=self.recv.at[self.count],
            device_id=device,
            device_id_type=MESH,
        )
        copy.start()
        self.count += 1
        assert self.count <= N_COPIES
        self.started.append(copy)
        return copy

    def drain(self, keep=0):
        while len(self.started) > keep:
            self.started.pop(0).wait_send()


def block_kernel(
    image_count, prompt_count,
    enc_own, mod_video, mod_text, enc_gain, final_gain, query_gain, key_gain, text_gain,
    video, w_qkv, gate_t, up_t, down, w_in, w_kv,
    out_ref,
    video_v, q_ref, kv_ref, text_ref, acc_ref, top_ref, staged,
    tok0, tok1, tok2, tok3, tok4, w_two, g_v, u_v, d_v, wi_v, wk_v,
    xq, xkv, granules, rows_v, normed_v, term_a, r_term_a, term_b, r_term_b, half_f, half_b,
    r_half, sum_b, r_sum_b, part, r_part,
    gain_v, proj, r_proj, proj_z, r_projz, cond, cond_mod,
    send, recv, out_send, out_recv, local_sem,
):
    g, y, h = lax.axis_index("grp"), lax.axis_index("blk"), lax.axis_index("head")
    z, X = h // 2, h % 2
    core = g % 2
    z_at = lambda dz: (g, y, ((z + dz) % 8) * 2 + X)
    y_at = lambda dy: (g, (y + dy) % 4, h)
    x_at = (g, y, z * 2 + (1 - X))
    w_at = ((g + 2) % 4, y, z * 2 + (1 - X))
    core_at = (g + 1 - 2 * core, y, h)

    def owner(k):
        c, x_rel = k % 8, k // 8
        offset = (c % 2) * (8 - (c + 1) // 2) + (1 - c % 2) * (c // 2)
        return (g, y, ((z + offset) % 8) * 2 + (X + x_rel) % 2)

    peers = [owner(k) for k in range(1, 16)] + [y_at(i) for i in range(1, 4)] + [w_at, core_at]

    loads = [
        pltpu.make_async_copy(src, dst, local_sem.at[i])
        for i, (src, dst) in enumerate(
            [(video, video_v), (w_qkv, w_two.at[0]), (gate_t, g_v), (up_t, u_v), (down, d_v), (w_in, wi_v.at[X]), (w_kv, wk_v)]
        )
    ]
    for load in loads:
        load.start()

    barrier = pltpu.get_barrier_semaphore()
    for peer in peers:
        pl.semaphore_signal(barrier, inc=1, device_id=peer, device_id_type=MESH)
    pl.semaphore_wait(barrier, len(peers))

    links = Links(send, recv)
    toks = [tok0, tok1, tok2, tok3, tok4]
    flight = {}

    def landed(name):
        for copy in flight[name]:
            copy.wait_recv()

    seen = set()

    def once(name):
        if name not in seen:
            seen.add(name)
            landed(name)

    def to_y(src, dst):
        return [links.start(src((y + i) % 4), dst(i), y_at(i)) for i in (1, 3, 2)]

    def to_sides(block):
        return [links.start(block, block, y_at(1)), links.start(block, block, y_at(3))]

    def to_z(src, dst):
        return [links.start(src((z + i) % 8), dst(i), z_at(i)) for i in (1, 7, 2, 6, 3, 5, 4)]

    def modulate_video(part):
        if part == 0:
            loads[0].wait()
        scale, shift = 1.0 + mod_video[1:2, :], mod_video[0:1, :]

        def modulate(i, _):
            at = pl.ds(pl.multiple_of(64 * part + i * 16, 16), 16)
            v = video_v[at, :].astype(F32)
            c = v - jnp.mean(v, axis=-1, keepdims=True)
            n = c * lax.rsqrt(jnp.mean(c * c, axis=-1, keepdims=True) + EPS)
            tok0[at, :] = (n * scale + shift).astype(BF16)
            return 0

        lax.fori_loop(0, 4, modulate, 0)

    def ring(step, part):
        at, low, high = pl.ds(64 * part, 64), 64 * part, 128 + 64 * part
        back = tok0.at[at] if step == 1 else toks[step - 1].at[pl.ds(high, 64)]
        copies = []
        if step < 4 or part == 0:
            copies.append(links.start(toks[step - 1].at[at], toks[step].at[at], z_at(1)))
        if step < 4:
            copies.append(links.start(back, toks[step].at[pl.ds(high, 64)], z_at(7)))
        elif part == 1:
            copies.append(links.start(back, tok4.at[at], z_at(7)))
        flight["tok", step, part] = copies

    def arrive(step, part):
        landed(("tok", step, part))
        if step < 4:
            ring(step + 1, part)

    other = w_two.at[1]

    def eighth(block, start=0, count=D // 8):
        first = (2 * block + core) * (D // 8) + start
        return other.at[pl.ds(pl.multiple_of(first, D // 16), count)]

    def to_core(*parts):
        return [links.start(part, part, core_at) for part in parts]

    def weights_x():
        mine = pl.ds(pl.multiple_of((2 * y + core) * (D // 8), D // 8), D // 8)
        flight["w_x"] = [links.start(w_qkv.at[mine], other.at[mine], w_at)]

    def weights_y():
        landed("w_x")
        flight["w_y"] = to_sides(eighth(y))
        flight["w_core"] = to_core(eighth(y))

    def weights_far():
        landed("w_y")
        below, above = (y + 3) % 4, (y + 1) % 4
        low, high = eighth(below, 0, D // 16), eighth(above, D // 16, D // 16)
        flight["w_far"] = [links.start(low, low, y_at(1)), links.start(high, high, y_at(3))]
        flight["w_core"] += to_core(eighth(below), eighth(above))

    def weights_core():
        landed("w_far")
        flight["w_core"] += to_core(eighth((y + 2) % 4))

    def project(step, which):
        first, count = STEP_CHUNKS[step]
        mixed = dot(toks[step][...], w_two[which])
        q = rms(mixed[:, :HD], query_gain[...]).astype(BF16)
        k = rms(mixed[:, HD : 2 * HD], key_gain[...]).astype(BF16)
        v = mixed[:, 2 * HD :].astype(BF16)
        for i in range(count):
            at = slice(i * 128, (i + 1) * 128)
            if which == 0:
                q_ref[0, first + i] = q[at]
                kv_ref[0, 0, first + i, 0] = k[at]
                kv_ref[0, 0, first + i, 1] = v[at]
            else:
                xq[first + i] = q[at]
                xkv[first + i, 0] = k[at]
                xkv[first + i, 1] = v[at]

    def spread(step, x_rel):
        chunks = pl.ds(*STEP_CHUNKS[step])
        if x_rel:
            landed(("x", step))
        mine = kv_ref.at[0, x_rel, chunks]
        flight["kv", step, x_rel] = [
            links.start(mine, kv_ref.at[3, x_rel, chunks], y_at(1)),
            links.start(mine, kv_ref.at[1, x_rel, chunks], y_at(3)),
        ]
        if step in DIRECT:
            last = links.start(mine, kv_ref.at[2, x_rel, chunks], y_at(2))
            flight["far", step, x_rel] = flight["kv", step, x_rel] + [last]

    def relay(step, x_rel):
        chunks = pl.ds(*STEP_CHUNKS[step])
        landed(("kv", step, x_rel))
        far = kv_ref.at[2, x_rel, chunks]
        flight["far", step, x_rel] = [
            links.start(kv_ref.at[3, x_rel, chunks, 0], far.at[:, 0], y_at(1)),
            links.start(kv_ref.at[1, x_rel, chunks, 1], far.at[:, 1], y_at(3)),
        ]

    def own_head(step):
        if step == 0:
            loads[1].wait()
        project(step, 0)

    def other_head(step):
        once("w_core")
        chunks = pl.ds(*STEP_CHUNKS[step])
        project(step, 1)
        flight["q", step] = [links.start(xq.at[chunks], q_ref.at[1, chunks], x_at)]
        flight["x", step] = [links.start(xkv.at[chunks], kv_ref.at[0, 1, chunks], x_at)]

    def enc_z():
        rows = enc_own[...].astype(F32)
        pieces = [rows[:, 512 * j : 512 * j + 512] for j in range(8)]
        granules[y, X, z] = jnp.concatenate(pieces, axis=0).astype(BF16)
        flight["enc_z"] = to_z(lambda _: granules.at[y, X, z], lambda _: granules.at[y, X, z])

    def enc_x():
        landed("enc_z")
        flight["enc_x"] = [links.start(granules.at[y, X], granules.at[y, X], x_at)]

    def enc_y():
        landed("enc_x")
        mine = granules.at[y]
        flight["enc_y"] = [links.start(mine, mine, y_at(1)), links.start(mine, mine, y_at(3))]

    def enc_far():
        landed("enc_y")
        low, high = granules.at[(y + 3) % 4, 0], granules.at[(y + 1) % 4, 1]
        flight["enc_far"] = [links.start(low, low, y_at(1)), links.start(high, high, y_at(3))]

    w_in_half = pl.ds(pl.multiple_of(32 * core, 32), 32)

    def gains_x():
        gain = jnp.concatenate([final_gain[...], jnp.zeros((1, 64), F32)], axis=1)
        gain_v[X] = jnp.broadcast_to(gain, (8, 128))
        flight["gains"] = [
            links.start(gain_v.at[X], gain_v.at[X], x_at),
            links.start(w_in.at[w_in_half], wi_v.at[X, w_in_half], x_at),
        ]

    def gains_core():
        landed("gains")
        half = wi_v.at[1 - X, w_in_half]
        flight["gains_core"] = [links.start(half, half, core_at)]

    def feed_forward():
        landed("enc_far")
        out_at = lax.broadcasted_iota(jnp.int32, (256, 256), 0)
        in_at = lax.broadcasted_iota(jnp.int32, (256, 256), 1)
        source = out_at % 32 // 2 * 16 + out_at // 32 * 2 + out_at % 2
        order = (in_at == source).astype(F32).astype(BF16)
        for b in range(4):
            ordered = dot(order, granules[b].reshape(256, 512)).astype(BF16)
            for j in range(8):
                for x in (0, 1):
                    rows_v[64 * x + 16 * b : 64 * x + 16 * b + 16, 512 * j : 512 * j + 512] = ordered[
                        32 * j + 16 * x : 32 * j + 16 * x + 16
                    ]

        def normalize(i, _):
            at = pl.ds(pl.multiple_of(i * 16, 16), 16)
            v = rows_v[at, :].astype(F32)
            normed_v[at, :] = rms(v, enc_gain[...]).astype(BF16)
            return 0

        lax.fori_loop(0, 8, normalize, 0)
        loads[2].wait()
        loads[3].wait()
        gate = dot_t(normed_v[...], g_v[...])
        upward = dot_t(normed_v[...], u_v[...])
        hidden = (gate / (1.0 + jnp.exp(-gate)) * upward).astype(BF16)
        loads[4].wait()
        for b in range(4):
            product = dot(hidden, d_v[:, 1024 * b : 1024 * b + 1024]).astype(BF16)
            term_a[b] = product[:, :512]
            term_b[0, b] = product[:64, 512:]
            term_b[1, b] = product[64:, 512:]
        flight["sum_a"] = to_y(lambda b: term_a.at[b], lambda i: r_term_a.at[i - 1])
        flight["sum_b"] = [links.start(term_b.at[1 - X], r_term_b, x_at)]

    def sum_xa():
        landed("sum_a")
        total = term_a[y].astype(F32)
        for i in range(3):
            total = total + r_term_a[i].astype(F32)
        for x in (0, 1):
            half_f[x] = total[64 * x : 64 * x + 64]
            half_b[x] = total[64 * x : 64 * x + 64].astype(BF16)
        flight["sum_xa"] = [links.start(half_b.at[1 - X], r_half, x_at)]

    def sum_yb():
        landed("sum_b")
        for b in range(4):
            sum_b[b] = (term_b[X, b].astype(F32) + r_term_b[b].astype(F32)).astype(BF16)
        flight["sum_yb"] = to_y(lambda b: sum_b.at[b], lambda i: r_sum_b.at[i - 1])

    def sum_z():
        landed("sum_xa")
        landed("sum_yb")
        total = half_f[X] + r_half[...].astype(F32)
        for i in range(4):
            part[i] = total[:, 128 * i : 128 * i + 128].astype(BF16)
        total = sum_b[y].astype(F32)
        for i in range(3):
            total = total + r_sum_b[i].astype(F32)
        for i in range(4):
            part[4 + i] = total[:, 128 * i : 128 * i + 128].astype(BF16)
        flight["sum_z"] = to_z(lambda b: part.at[b], lambda i: r_part.at[i - 1])

    def refine():
        landed("sum_z")
        total = part[z].astype(F32)
        for i in range(7):
            total = total + r_part[i].astype(F32)
        column = pl.multiple_of(y * 1024 + z * 128, 128)
        own_rows = pl.ds(pl.multiple_of(X * 64, 64), 64)
        enc_out = total + rows_v[own_rows, pl.ds(column, 128)].astype(F32)
        squares = jnp.sum(enc_out * enc_out, axis=-1, keepdims=True)
        landed("gains_core")
        gain = jnp.concatenate([gain_v[0][:1, :64], gain_v[1][:1, :64]], axis=1)
        scaled = (enc_out * gain).astype(BF16)
        loads[5].wait()
        wide = jnp.broadcast_to(squares, (64, 128)).astype(BF16)
        for b in range(4):
            proj[b, :, D:] = wide[16 * b : 16 * b + 16]
        for i in range(6):
            weights = wi_v[:, :, 512 * i : 512 * i + 512].reshape(128, 512)
            product = dot(scaled, weights).astype(BF16)
            for b in range(4):
                proj[b, :, 512 * i : 512 * i + 512] = product[16 * b : 16 * b + 16]
        flight["ref_y"] = to_y(lambda b: proj.at[b], lambda i: r_proj.at[i - 1])

    def refine_z():
        landed("ref_y")
        total = proj[y].astype(F32)
        for i in range(3):
            total = total + r_proj[i].astype(F32)
        for i in range(8):
            proj_z[i, :, :384] = total[:, 384 * i : 384 * i + 384].astype(BF16)
            proj_z[i, :, 384:] = total[:, D:].astype(BF16)
        flight["ref_z"] = to_z(lambda b: proj_z.at[b], lambda i: r_projz.at[i - 1])

    def refine_all():
        landed("ref_z")
        total = proj_z[z].astype(F32)
        for i in range(7):
            total = total + r_projz[i].astype(F32)
        cond[z] = (total[:, :384] * lax.rsqrt(total[:, 384:385] / ED + EPS)).astype(BF16)
        flight["cond"] = to_z(lambda _: cond.at[z], lambda _: cond.at[z])

    def modulate_x():
        landed("cond")
        total = jnp.zeros((16, 1), F32)
        for i in range(8):
            total = total + jnp.sum(cond[i].astype(F32), axis=-1, keepdims=True)
        mean = total / D
        total = jnp.zeros((16, 1), F32)
        for i in range(8):
            c = cond[i].astype(F32) - mean
            total = total + jnp.sum(c * c, axis=-1, keepdims=True)
        inverse = lax.rsqrt(total / D + EPS)
        for i in range(8):
            at = slice(384 * i, 384 * i + 384)
            c = (cond[i].astype(F32) - mean) * inverse
            cond_mod[X, :, at] = (c * (1.0 + mod_text[1:2, at]) + mod_text[0:1, at]).astype(BF16)
        flight["cond_mod"] = [links.start(cond_mod.at[X], cond_mod.at[X], x_at)]

    def text():
        landed("cond_mod")
        loads[6].wait()
        text_kv = dot(cond_mod[...].reshape(32, D), wk_v[...])
        text_ref[y, 0] = rms(text_kv[:, :HD], text_gain[...]).astype(BF16)
        text_ref[y, 1] = text_kv[:, HD:].astype(BF16)
        flight["text"] = to_y(lambda _: text_ref.at[y], lambda _: text_ref.at[y])

    factor = HD ** (-0.5) * 1.4426950408889634

    def dead_bias():
        at = lax.broadcasted_iota(jnp.int32, (1, 128), 1)
        row = at // 32 * 32 + at // 2 % 8 * 4 + at // 16 % 2 * 2 + at % 2
        end = jnp.where(row < IMG_ROWS, image_count[0], IMG_ROWS + prompt_count[0])
        return jnp.where(row < end, 0.0, NEG)

    def attend(i, tiles, fresh, last):
        q = q_ref[:, i].reshape(256, 128)
        tiles = list(tiles) + (["text"] if last else [])

        def scores_of(n):
            if n == "text":
                return dot_t(q, text_ref[:, 0].reshape(128, 128)) * factor + dead_bias()
            return dot_t(q, kv_ref[:, :, n, 0].reshape(1024, 128)) * factor

        def values_of(n):
            if n == "text":
                v = text_ref[:, 1].reshape(128, 128)
            else:
                v = kv_ref[:, :, n, 1].reshape(1024, 128)
            return jnp.concatenate([v, jnp.ones(v.shape, BF16)], axis=1)

        highest = acc = None
        if not fresh:
            highest, acc = top_ref[i][:, :1], acc_ref[i]
        s = scores_of(tiles[0])
        for at, n in enumerate(tiles):
            following = scores_of(tiles[at + 1]) if at + 1 < len(tiles) else None
            top = jnp.max(s, axis=-1, keepdims=True)
            if highest is not None:
                top = jnp.maximum(highest, top)
            product = dot(jnp.exp2(s - top).astype(BF16), values_of(n))
            acc = product if highest is None else acc * jnp.exp2(highest - top) + product
            highest, s = top, following
        if not last:
            top_ref[i] = jnp.broadcast_to(highest, (256, 128))
            acc_ref[i] = acc
            return
        out = (acc[:, :HD] / acc[:, HD:]).astype(BF16)
        staged[i] = out[:128]
        staged[8 + i] = out[128:]
        deliver(8 + i).start()

        @pl.when(i > 0)
        def _():
            deliver(i).start()

    def queries(first, end, tiles, fresh, last=False):
        def body(i, _):
            attend(end - 1 - i, tiles, fresh, last)
            return 0

        lax.fori_loop(0, end - first, body, 0)

    def attend_to(first, end, key_first, key_end, last=False):
        for step, (chunk, _) in enumerate(STEP_CHUNKS):
            if chunk < key_end:
                once(("far", step, 0))
                once(("far", step, 1))
            if chunk < end:
                once(("q", step))
        if last:
            once("text")
        queries(first, end, range(key_first, key_end), key_first == 0, last)

    columns = pl.ds(pl.multiple_of(h * 128, 128), 128)

    def deliver(k):
        return pltpu.make_async_remote_copy(
            src_ref=staged.at[k],
            dst_ref=out_ref.at[:, columns],
            send_sem=out_send.at[k],
            recv_sem=out_recv.at[k],
            device_id=owner(k),
            device_id_type=MESH,
        )

    def drain():
        links.drain(24)

    def finish():
        own = pltpu.make_async_copy(staged.at[0], out_ref.at[:, columns], local_sem.at[7])
        own.start()
        own.wait()
        links.drain()
        for k in range(1, 16):
            deliver(k).wait()

    stages = locals()
    for name, *step in PLAN:
        stages[name](*step)


PLAN = (
    ("enc_z",), ("modulate_video", 0), ("ring", 1, 0), ("enc_x",), ("modulate_video", 1),
    ("ring", 1, 1), ("own_head", 0), ("spread", 0, 0), ("weights_x",), ("enc_y",), ("weights_y",),
    ("arrive", 1, 0), ("enc_far",), ("arrive", 1, 1), ("weights_far",), ("feed_forward",),
    ("own_head", 1), ("arrive", 2, 0), ("spread", 1, 0), ("weights_core",), ("other_head", 0),
    ("other_head", 1), ("relay", 0, 0), ("arrive", 2, 1), ("sum_yb",), ("other_head", 2),
    ("own_head", 2), ("spread", 2, 0), ("spread", 0, 1), ("spread", 1, 1), ("sum_xa",),
    ("gains_x",), ("spread", 2, 1), ("sum_z",), ("relay", 1, 0), ("relay", 1, 1), ("gains_core",),
    ("relay", 0, 1), ("drain",), ("arrive", 3, 0), ("arrive", 3, 1), ("other_head", 3),
    ("relay", 2, 1), ("own_head", 3), ("relay", 2, 0), ("refine",), ("attend_to", 0, 3, 0, 3),
    ("spread", 3, 0), ("attend_to", 3, 5, 0, 5), ("spread", 3, 1), ("refine_z",), ("drain",),
    ("arrive", 4, 0), ("attend_to", 5, 6, 0, 5), ("attend_to", 6, 7, 0, 5), ("arrive", 4, 1),
    ("refine_all",), ("other_head", 4), ("own_head", 4), ("attend_to", 0, 3, 3, 5),
    ("spread", 4, 0), ("modulate_x",), ("attend_to", 5, 7, 5, 7), ("spread", 4, 1),
    ("attend_to", 7, 8, 0, 7), ("text",), ("attend_to", 0, 5, 5, 7), ("drain",),
    ("attend_to", 0, 8, 7, 8, True), ("finish",),
)


def local(
    enc_states, image_count, prompt_count, enc_gain, enc_gate, enc_up, enc_down, final_gain, w_in,
    mod_text, mod_video, w_kv_text, w_qkv, query_gain, key_gain, text_key_gain, video_states,
):
    vmem, hbm = pl.BlockSpec(memory_space=pltpu.VMEM), pl.BlockSpec(memory_space=pl.ANY)
    smem = pl.BlockSpec(memory_space=pltpu.SMEM)
    row = lambda v: v.reshape(1, -1)
    return pl.pallas_call(
        block_kernel,
        out_shape=jax.ShapeDtypeStruct((128, 2048), BF16),
        in_specs=[smem] * 2 + [vmem] * 8 + [hbm] * 7,
        out_specs=vmem,
        scratch_shapes=[
            pltpu.VMEM((128, D), BF16),
            pltpu.VMEM((2, 8, 128, 128), BF16),
            pltpu.VMEM((4, 2, 8, 2, 128, 128), BF16),
            pltpu.VMEM((4, 2, 32, 128), BF16),
            pltpu.VMEM((8, 256, 256), F32),
            pltpu.VMEM((8, 256, 128), F32),
            pltpu.VMEM((16, 128, 128), BF16),
            pltpu.VMEM((128, D), BF16),
            pltpu.VMEM((256, D), BF16),
            pltpu.VMEM((256, D), BF16),
            pltpu.VMEM((256, D), BF16),
            pltpu.VMEM((128, D), BF16),
            pltpu.VMEM((2, D, 3 * HD), BF16),
            pltpu.VMEM((224, ED), BF16),
            pltpu.VMEM((224, ED), BF16),
            pltpu.VMEM((224, ED), BF16),
            pltpu.VMEM((2, 64, D), BF16),
            pltpu.VMEM((D, 2 * HD), BF16),
            pltpu.VMEM((8, 128, 128), BF16),
            pltpu.VMEM((8, 2, 128, 128), BF16),
            pltpu.VMEM((4, 2, 8, 16, 512), BF16),
            pltpu.VMEM((128, ED), BF16),
            pltpu.VMEM((128, ED), BF16),
            pltpu.VMEM((4, 128, 512), BF16),
            pltpu.VMEM((3, 128, 512), BF16),
            pltpu.VMEM((2, 4, 64, 512), BF16),
            pltpu.VMEM((4, 64, 512), BF16),
            pltpu.VMEM((2, 64, 512), F32),
            pltpu.VMEM((2, 64, 512), BF16),
            pltpu.VMEM((64, 512), BF16),
            pltpu.VMEM((4, 64, 512), BF16),
            pltpu.VMEM((3, 64, 512), BF16),
            pltpu.VMEM((8, 64, 128), BF16),
            pltpu.VMEM((7, 64, 128), BF16),
            pltpu.VMEM((2, 8, 128), F32),
            pltpu.VMEM((4, 16, D + 128), BF16),
            pltpu.VMEM((3, 16, D + 128), BF16),
            pltpu.VMEM((8, 16, 512), BF16),
            pltpu.VMEM((7, 16, 512), BF16),
            pltpu.VMEM((8, 16, 384), BF16),
            pltpu.VMEM((2, 16, D), BF16),
            pltpu.SemaphoreType.DMA((N_COPIES,)),
            pltpu.SemaphoreType.DMA((N_COPIES,)),
            pltpu.SemaphoreType.DMA((16,)),
            pltpu.SemaphoreType.DMA((16,)),
            pltpu.SemaphoreType.DMA((8,)),
        ],
        compiler_params=pltpu.CompilerParams(
            collective_id=0, has_side_effects=True, vmem_limit_bytes=58 * 2**20
        ),
        name="block",
    )(
        image_count, prompt_count, enc_states, mod_video[0], mod_text[0], row(enc_gain),
        row(final_gain), row(query_gain), row(key_gain), row(text_key_gain),
        video_states, w_qkv[:, 0, :], enc_gate.T, enc_up.T, enc_down, w_in, w_kv_text[:, 0, :],
    )


def solution(mesh):
    placed = (
        P(("grp", "blk", "head"), None),
        P("grp"),
        P("grp"),
        P(),
        P(None, ("blk", "head")),
        P(None, ("blk", "head")),
        P(("blk", "head"), None),
        P(("blk", "head")),
        P(("blk", "head"), None),
        P("grp", None, None),
        P("grp", None, None),
        P(None, "head", None),
        P(None, "head", None),
        P(),
        P(),
        P(),
        P(("grp", "blk", "head"), None),
    )
    return jax.shard_map(
        local,
        mesh=mesh,
        in_specs=placed,
        out_specs=P(("grp", "blk", "head"), None),
        check_vma=False,
    )
```
